32 devices in a mesh: groups: 2 (over y), seq: 16 (over z, x, core).
Axes of the slice: x: 2, y: 2, z: 4, core: 2. Of those that a mesh axis runs over, the one named last changes fastest.
Arguments:
- queries: bfloat16 [12288, 2048], P(('groups', 'seq')), parts along dimension 0, may hold values from -6 to 6
- keys: bfloat16 [12288, 2048], P(('groups', 'seq')), parts along dimension 0, may hold values from -6 to 6
- values: bfloat16 [12288, 2048], P(('groups', 'seq')), parts along dimension 0, may hold values from -6 to 6
- out_grad: bfloat16 [12288, 2048], P(('groups', 'seq')), parts along dimension 0, may hold values from -6 to 6
Outputs:
- grad_queries: bfloat16 [12288, 2048], P(('groups', 'seq')), parts along dimension 0
- grad_keys: bfloat16 [12288, 2048], P(('groups', 'seq')), parts along dimension 0
- grad_values: bfloat16 [12288, 2048], P(('groups', 'seq')), parts along dimension 0
The draws below stay inside these ranges and needn't reach their ends.
There are 2 independent parts, one for each index of `groups`. The reference program is written for one: setup_inputs(seed, part) draws one part's arguments, and reference() takes and returns one part's arrays. A program takes and returns all parts, laid end to end along the dimension named above; each array names one. Nothing has to cross between parts.
All inputs are finite; a program needn't handle non-finite values.
Results may differ from the reference program's by a relative error of at most 0.0049.
Values sent between devices are 32-bit elements; how exact they have to be, the bound alone decides.
No kernel may reach another device: no remote copies, remote signals or barrier semaphores. Data moves between devices by JAX's collectives and lax.ppermute only.
A program may use at most 64 MiB of HBM per device.

```python
import jax
import jax.numpy as jnp
from jax import lax

HEADS = 16
HD = 128
TOK_DEV = 384
WIDTH = 2048
LEN = 6144


def steps_of(own_key, extent, cuts, low, top_value):
    gain, own = 1.0, jax.random.fold_in(own_key, 6)
    for axis_at, parts in cuts:
        heights = jnp.exp(jax.random.uniform(jax.random.fold_in(own, axis_at), (parts,), jnp.float32, low / len(cuts), top_value / len(cuts)))
        gain = gain * jnp.repeat(heights, extent[axis_at] // parts).reshape([-1 if axis == axis_at else 1 for axis in range(len(extent))])
    return gain


def scatter_about(rng, shape, deviation, limit, shards=(), dtype=jnp.bfloat16):
    loudness = steps_of(rng, shape, shards, -0.22, 0.18) if shards else 1.0
    values = jax.random.normal(rng, shape, jnp.float32) * deviation * loudness
    return jnp.minimum(jnp.maximum(values, -limit), limit).astype(dtype)


def setup_inputs(seed: int = 0, part: int = 0) -> dict:
    key_list = jax.random.split(jax.random.key(seed), 5)
    part_splits = jax.random.split(jax.random.fold_in(key_list[4], part), 5)
    queries = scatter_about(part_splits[0], (LEN, WIDTH), 1.0, 6.0, ((0, 16),))
    keys = scatter_about(part_splits[1], (LEN, WIDTH), 1.0, 6.0, ((0, 16),))
    values = scatter_about(part_splits[2], (LEN, WIDTH), 1.0, 6.0, ((0, 16),))
    out_grad = scatter_about(part_splits[3], (LEN, WIDTH), 1.0, 6.0, ((0, 16),))
    return {"queries": queries, "keys": keys, "values": values, "out_grad": out_grad}


def block_grads(qb, kb, vb, gb, kv_state, qg_state, scale):
    qf = qb.astype(jnp.float32)
    kf = kb.astype(jnp.float32)
    vf = vb.astype(jnp.float32)
    gf = gb.astype(jnp.float32)
    rows = qb.shape[0]
    lower = jnp.tril(jnp.ones((rows, rows), jnp.float32))
    weights = (jnp.einsum('thd,shd->hts', qf, kf) * scale * lower).astype(jnp.bfloat16).astype(jnp.float32)
    grad_scores = (jnp.einsum('thd,shd->hts', gf, vf) * scale * lower).astype(jnp.bfloat16).astype(jnp.float32)
    kvs = kv_state.astype(jnp.float32)
    qgs = qg_state.astype(jnp.float32)
    grad_q = jnp.einsum('hts,shd->thd', grad_scores, kf) + scale * jnp.einsum('the,hde->thd', gf, kvs)
    grad_k = jnp.einsum('hts,thd->shd', grad_scores, qf) + scale * jnp.einsum('she,hde->shd', vf, qgs)
    grad_v = jnp.einsum('hts,the->she', weights, gf) + scale * jnp.einsum('shd,hde->she', kf, qgs)
    return (grad_q.astype(jnp.bfloat16), grad_k.astype(jnp.bfloat16), grad_v.astype(jnp.bfloat16))

def reference(queries, keys, values, out_grad):
    blocks = LEN // TOK_DEV
    scale = 1.0 / jnp.sqrt(jnp.float32(HD * LEN))
    shape4 = (blocks, TOK_DEV, HEADS, HD)
    qs = queries.reshape(shape4)
    ks = keys.reshape(shape4)
    vs = values.reshape(shape4)
    gs = out_grad.reshape(shape4)
    kv_local = jnp.einsum('bshd,bshe->bhde', ks.astype(jnp.float32), vs.astype(jnp.float32))
    qg_local = jnp.einsum('bshd,bshe->bhde', qs.astype(jnp.float32), gs.astype(jnp.float32))

    def forward(carry, term):
        return (carry + term, carry)
    zeros = jnp.zeros((HEADS, HD, HD), jnp.float32)
    _, kv_state = lax.scan(forward, zeros, kv_local)
    _, qg_state = lax.scan(forward, zeros, qg_local, reverse=True)
    kv_state = kv_state.astype(jnp.bfloat16)
    qg_state = qg_state.astype(jnp.bfloat16)

    def one_block(items):
        return block_grads(items[0], items[1], items[2], items[3], items[4], items[5], scale)
    grad_q, grad_k, grad_v = lax.map(one_block, (qs, ks, vs, gs, kv_state, qg_state))
    return (grad_q.reshape(LEN, WIDTH), grad_k.reshape(LEN, WIDTH), grad_v.reshape(LEN, WIDTH))
```

```python
import functools

import jax
import jax.numpy as jnp
from jax import lax
from jax.experimental import pallas as pl
from jax.experimental.pallas import tpu as pltpu
from jax.sharding import PartitionSpec as P

HD = 128
CHUNKS = 2
F32 = jnp.float32
BF16 = jnp.bfloat16
VMEM_LIMIT = 40 * 1024 * 1024


def dot(a, b, dims):
    return lax.dot_general(a, b, (dims, ((), ())), preferred_element_type=F32)


def params():
    return pltpu.CompilerParams(vmem_limit_bytes=VMEM_LIMIT)


def state_kernel(heads, a_ref, b_ref, out_ref):
    for h in range(heads):
        cols = slice(h * HD, (h + 1) * HD)
        out_ref[h] = dot(a_ref[:, cols], b_ref[:, cols], ((0,), (0,)))


def local_state(a, b, first, heads):
    rows = a.shape[0]
    per = min(heads, 4)
    block = pl.BlockSpec((rows, per * HD), lambda i: (0, first // per + i))
    return pl.pallas_call(
        functools.partial(state_kernel, per),
        grid=(heads // per,),
        out_shape=jax.ShapeDtypeStruct((heads, HD, HD), F32),
        in_specs=[block, block],
        out_specs=pl.BlockSpec((per, HD, HD), lambda i: (i, 0, 0)),
        compiler_params=params(),
        cost_estimate=pl.CostEstimate(
            flops=2 * heads * rows * HD * HD, bytes_accessed=4 * heads * rows * HD, transcendentals=0
        ),
    )(a, b)


def within_kernel(heads, scale, q_ref, k_ref, v_ref, g_ref, dq_ref, dk_ref, dv_ref):
    rows = q_ref.shape[0]
    at = lax.broadcasted_iota(jnp.int32, (rows, rows), 0)
    upto = lax.broadcasted_iota(jnp.int32, (rows, rows), 1) <= at
    for h in range(heads):
        cols = slice(h * HD, (h + 1) * HD)
        q, k, v, g = q_ref[:, cols], k_ref[:, cols], v_ref[:, cols], g_ref[:, cols]
        weights = jnp.where(upto, dot(q, k, ((1,), (1,))) * scale, 0.0).astype(BF16)
        scores = jnp.where(upto, dot(g, v, ((1,), (1,))) * scale, 0.0).astype(BF16)
        dq_ref[:, cols] = dot(scores, k, ((1,), (0,))).astype(BF16)
        dk_ref[:, cols] = dot(scores, q, ((0,), (0,))).astype(BF16)
        dv_ref[:, cols] = dot(weights, g, ((0,), (0,))).astype(BF16)


def within(q, k, v, g, first, heads, scale):
    rows = q.shape[0]
    per = min(heads, 2)
    block = pl.BlockSpec((rows, per * HD), lambda i: (0, first // per + i))
    out = pl.BlockSpec((rows, per * HD), lambda i: (0, i))
    return pl.pallas_call(
        functools.partial(within_kernel, per, scale),
        grid=(heads // per,),
        out_shape=[jax.ShapeDtypeStruct((rows, heads * HD), BF16)] * 3,
        in_specs=[block] * 4,
        out_specs=[out] * 3,
        compiler_params=params(),
        cost_estimate=pl.CostEstimate(
            flops=10 * heads * rows * rows * HD, bytes_accessed=14 * heads * rows * HD, transcendentals=0
        ),
    )(q, k, v, g)


def final_kernel(heads, scale, k_ref, v_ref, g_ref, kv_ref, qg_ref, pq_ref, pk_ref, pv_ref, dq_ref, dk_ref, dv_ref):
    for h in range(heads):
        cols = slice(h * HD, (h + 1) * HD)
        kv, qg = kv_ref[h].astype(BF16), qg_ref[h].astype(BF16)
        dq_ref[:, cols] = (pq_ref[:, cols].astype(F32) + scale * dot(g_ref[:, cols], kv, ((1,), (1,)))).astype(BF16)
        dk_ref[:, cols] = (pk_ref[:, cols].astype(F32) + scale * dot(v_ref[:, cols], qg, ((1,), (1,)))).astype(BF16)
        dv_ref[:, cols] = (pv_ref[:, cols].astype(F32) + scale * dot(k_ref[:, cols], qg, ((1,), (0,)))).astype(BF16)


def final(k, v, g, kv, qg, partials, scale):
    rows = k.shape[0]
    heads = kv.shape[0]
    per = min(heads, 2)
    block = pl.BlockSpec((rows, per * HD), lambda i: (0, i))
    state = pl.BlockSpec((per, HD, HD), lambda i: (i, 0, 0))
    return pl.pallas_call(
        functools.partial(final_kernel, per, scale),
        grid=(heads // per,),
        out_shape=[jax.ShapeDtypeStruct((rows, heads * HD), BF16)] * 3,
        in_specs=[block] * 3 + [state] * 2 + [block] * 3,
        out_specs=[block] * 3,
        compiler_params=params(),
        cost_estimate=pl.CostEstimate(
            flops=6 * heads * rows * HD * HD, bytes_accessed=18 * heads * rows * HD, transcendentals=0
        ),
    )(k, v, g, kv, qg, *partials)


def local(seq, queries, keys, values, out_grad):
    rows = queries.shape[0]
    heads = queries.shape[1] // HD
    scale = float(1.0 / (HD * rows * seq) ** 0.5)
    at = lax.axis_index("seq")
    later = at % 2 == 1
    second = (at // 2 + at) % 2 == 0
    second = jnp.where(later, (at // 2) % 2 == 1, (at // 2) % 2 == 0)

    core_pairs = [(i, i ^ 1) for i in range(seq)]
    chip_pairs = [(i, i ^ 2) for i in range(seq)]

    def shift(value, by):
        pairs = []
        for i in range(seq):
            j = i + 4 * by if i % 2 else i - 4 * by
            if 0 <= j < seq:
                pairs.append((i, j))
        return lax.ppermute(value, "seq", pairs)

    size = heads // CHUNKS
    half = size // 2
    kvs, qgs = [], []
    for chunk in range(CHUNKS):
        first = chunk * size
        kv = local_state(keys, values, first, size)
        qg = local_state(queries, out_grad, first, size)
        mine = jnp.where(later, kv, qg)
        other = lax.ppermute(jnp.where(later, qg, kv), "seq", core_pairs)
        chip = mine + other
        kept = jnp.where(second, chip[half:], chip[:half])
        partner = lax.ppermute(jnp.where(second, chip[:half], chip[half:]), "seq", chip_pairs)
        plane = kept + partner
        before = shift(plane, 1)
        window = plane + before
        by = 2
        while 4 * by < seq:
            more = shift(window, by)
            before = before + more
            window = window + more
            by *= 2
        swapped = lax.ppermute(jnp.where(second, before, before + kept), "seq", chip_pairs)
        upto = jnp.concatenate(
            [jnp.where(second, swapped, before), jnp.where(second, before + partner, swapped)]
        )
        given = lax.ppermute(upto, "seq", core_pairs)
        here = upto + other
        kvs.append(jnp.where(later, here, given))
        qgs.append(jnp.where(later, given, here))

    partials = within(queries, keys, values, out_grad, 0, heads, scale)
    kv = jnp.concatenate(kvs)
    qg = jnp.concatenate(qgs)
    return tuple(final(keys, values, out_grad, kv, qg, partials, scale))


def solution(mesh):
    spec = P(("groups", "seq"), None)
    return jax.shard_map(
        functools.partial(local, mesh.shape["seq"]),
        mesh=mesh,
        in_specs=(spec,) * 4,
        out_specs=(spec,) * 3,
        check_vma=False,
    )
```

```python
import functools

import jax
import jax.numpy as jnp
from jax import lax
from jax.experimental import pallas as pl
from jax.experimental.pallas import tpu as pltpu
from jax.sharding import PartitionSpec as P

HD = 128
CHUNKS = (8, 8)
RADIX = 2
PIECE = 4
PLACES = (
    ((0, 0), ("kept", 1), ("plane", 0)),
    ((0, 1), ("kept", 1), ("plane", 0)),
    ((1, 0), ("kept", 1), ("scan", 0)),
    ((1, 1), ("kept", 1), ("scan", 0)),
)
F32 = jnp.float32
BF16 = jnp.bfloat16
VMEM_LIMIT = 24 * 1024 * 1024
VMEM_MOST = 46 * 1024 * 1024
ANY = pl.BlockSpec(memory_space=pl.ANY)
HBM = pl.BlockSpec(memory_space=pltpu.HBM)
VMEM = pl.BlockSpec(memory_space=pltpu.VMEM)


def dot(a, b, dims):
    return lax.dot_general(a, b, (dims, ((), ())), preferred_element_type=F32)


def cost(flops, size):
    return pl.CostEstimate(flops=flops, bytes_accessed=size, transcendentals=0)


def place():
    at = lax.axis_index("seq")
    core, chip = lax.rem(at, 2), lax.rem(at // 2, 2)
    return core == 1, core == chip


def first_kernel(size, q_ref, k_ref, v_ref, g_ref, other_ref, qv_ref, kv_ref, vv_ref, gv_ref, sem):
    later, second = place()
    width = q_ref.shape[1]
    cut = size * HD
    pieces = [(0, cut // 2), (cut // 2, cut // 2)] + ([(cut, width - cut)] if width > cut else [])

    def copies(j, source, target):
        made = []
        for n, (start, count) in enumerate(pieces):
            cols = pl.ds(start, count)
            made.append(pltpu.make_async_copy(source.at[:, cols], target.at[:, cols], sem.at[j, n]))
        return made

    q, k, v, g = (
        copies(j, source, target)
        for j, (source, target) in enumerate(((q_ref, qv_ref), (k_ref, kv_ref), (v_ref, vv_ref), (g_ref, gv_ref)))
    )

    def run(pair, refs, rest):
        for n in range(2):
            for copy in pair:
                copy[n].start()
        for copy in rest:
            for n in range(2):
                copy[n].start()
        for copy in (*rest, *pair):
            for n in range(2, len(pieces)):
                copy[n].start()
        half = size // 2
        turn = jnp.where(second, 0, half)
        for n in range(2):
            for copy in pair:
                copy[n].wait()
            for h in range(half):
                cols = slice((n * half + h) * HD, (n * half + h + 1) * HD)
                other_ref[lax.rem(n * half + turn, size) + h] = dot(refs[0][:, cols], refs[1][:, cols], ((0,), (0,)))
        for copy in rest:
            for n in range(2):
                copy[n].wait()
        for copy in (*rest, *pair):
            for n in range(2, len(pieces)):
                copy[n].wait()

    @pl.when(later)
    def _():
        run((q, g), (qv_ref, gv_ref), (k, v))

    @pl.when(jnp.logical_not(later))
    def _():
        run((k, v), (kv_ref, vv_ref), (q, g))


def first_state(arrays, size):
    rows, width = arrays[0].shape
    return pl.pallas_call(
        functools.partial(first_kernel, size),
        out_shape=[jax.ShapeDtypeStruct((size, HD, HD), F32)] + [jax.ShapeDtypeStruct((rows, width), BF16)] * 4,
        in_specs=[ANY] * 4,
        out_specs=[VMEM] * 5,
        scratch_shapes=[pltpu.SemaphoreType.DMA((4, 3))],
        compiler_params=pltpu.CompilerParams(vmem_limit_bytes=VMEM_MOST),
        cost_estimate=cost(2 * size * rows * HD * HD, 16 * rows * width),
    )(*arrays)


def other_kernel(size, q_ref, k_ref, v_ref, g_ref, out_ref):
    later, second = place()
    half = size // 2
    turn = jnp.where(second, 0, half)

    def run(a_ref, b_ref):
        for h in range(size):
            cols = slice(h * HD, (h + 1) * HD)
            at = lax.rem(h // half * half + turn, size) + h % half
            out_ref[at] = dot(a_ref[:, cols], b_ref[:, cols], ((0,), (0,)))

    @pl.when(later)
    def _():
        run(q_ref, g_ref)

    @pl.when(jnp.logical_not(later))
    def _():
        run(k_ref, v_ref)


def mine_kernel(size, q_ref, k_ref, v_ref, g_ref, other_ref, kept_ref, sent_ref):
    later, second = place()
    half = size // 2

    def run(pair, swap):
        refs = (sent_ref, kept_ref) if swap else (kept_ref, sent_ref)
        for h in range(size):
            cols = slice(h * HD, (h + 1) * HD)
            at = (h + (half if swap else 0)) % size
            value = dot(pair[0][:, cols], pair[1][:, cols], ((0,), (0,)))
            refs[h // half][h % half] = value + other_ref[at]

    for is_later, pair in ((True, (k_ref, v_ref)), (False, (q_ref, g_ref))):
        for swap in (True, False):
            pl.when(jnp.logical_and(later == is_later, second == swap))(functools.partial(run, pair, swap))


def other_state(arrays, first, size):
    rows = arrays[0].shape[0]
    block = pl.BlockSpec((rows, size * HD), lambda i: (0, first // size))
    return pl.pallas_call(
        functools.partial(other_kernel, size),
        grid=(1,),
        out_shape=jax.ShapeDtypeStruct((size, HD, HD), F32),
        in_specs=[block] * 4,
        out_specs=pl.BlockSpec((size, HD, HD), lambda i: (0, 0, 0)),
        compiler_params=pltpu.CompilerParams(vmem_limit_bytes=VMEM_LIMIT),
        cost_estimate=cost(2 * size * rows * HD * HD, 4 * size * rows * HD),
    )(*arrays)


def chip_state(arrays, other, first, size):
    rows = arrays[0].shape[0]
    half = jax.ShapeDtypeStruct((size // 2, HD, HD), F32)
    block = pl.BlockSpec((rows, size * HD), lambda i: (0, first // size))
    out = pl.BlockSpec((size // 2, HD, HD), lambda i: (0, 0, 0))
    return pl.pallas_call(
        functools.partial(mine_kernel, size),
        grid=(1,),
        out_shape=[half, half],
        in_specs=[block] * 4 + [pl.BlockSpec((size, HD, HD), lambda i: (0, 0, 0))],
        out_specs=[out, out],
        compiler_params=pltpu.CompilerParams(vmem_limit_bytes=VMEM_LIMIT),
        cost_estimate=cost(2 * size * rows * HD * HD, 4 * size * rows * HD),
    )(*arrays, other)


def sums_kernel(count, outs, work, *refs):
    values = work(*[ref[...] for ref in refs[:count]])
    for ref, value in zip(refs[-outs:], values):
        ref[...] = value


def sums(work, outs, values, after=()):
    return pl.pallas_call(
        functools.partial(sums_kernel, len(values), outs, work),
        out_shape=[jax.ShapeDtypeStruct(values[0].shape, F32)] * outs,
        in_specs=[VMEM] * len(values) + [ANY] * len(after),
        out_specs=[VMEM] * outs,
        compiler_params=pltpu.CompilerParams(vmem_limit_bytes=VMEM_LIMIT),
        cost_estimate=cost(values[0].size, 8 * values[0].size),
    )(*values, *after)


def within_kernel(heads, scale, q_ref, k_ref, v_ref, g_ref, *refs):
    dq_ref, dk_ref, dv_ref = refs[-3:]
    rows = q_ref.shape[0]
    at = lax.broadcasted_iota(jnp.int32, (rows, rows), 0)
    upto = lax.broadcasted_iota(jnp.int32, (rows, rows), 1) <= at
    for h in range(heads):
        cols = slice(h * HD, (h + 1) * HD)
        q, k, v, g = q_ref[:, cols], k_ref[:, cols], v_ref[:, cols], g_ref[:, cols]
        weights = jnp.where(upto, dot(q, k, ((1,), (1,))) * scale, 0.0).astype(BF16)
        scores = jnp.where(upto, dot(g, v, ((1,), (1,))) * scale, 0.0).astype(BF16)
        dq_ref[:, cols] = dot(scores, k, ((1,), (0,))).astype(BF16)
        dk_ref[:, cols] = dot(scores, q, ((0,), (0,))).astype(BF16)
        dv_ref[:, cols] = dot(weights, g, ((0,), (0,))).astype(BF16)


def within(arrays, first, size, start, heads, scale, held, after):
    rows = arrays[0].shape[0]
    per = min(heads, 2)
    block = pl.BlockSpec((rows, per * HD), lambda i: (0, (first + start) // per + i))
    out = pl.BlockSpec((rows, per * HD), lambda i: (0, start // per + i))
    return pl.pallas_call(
        functools.partial(within_kernel, per, scale),
        grid=(heads // per,),
        out_shape=[jax.ShapeDtypeStruct((rows, size * HD), BF16)] * 3,
        in_specs=[block] * 4 + [ANY] * len((*held, *after)),
        out_specs=[out] * 3,
        input_output_aliases={4 + j: j for j in range(len(held))},
        compiler_params=pltpu.CompilerParams(vmem_limit_bytes=VMEM_LIMIT),
        cost_estimate=cost(heads * rows * HD, heads * rows * HD),
    )(*arrays, *held, *after)


def final_kernel(per, half, scale, *refs):
    k_ref, v_ref, g_ref, pq_ref, pk_ref, pv_ref = refs[:6]
    low_ref, high_ref, kept_ref, swapped_ref, gkept_ref, gswapped_ref = refs[6:12]
    dq_ref, dk_ref, dv_ref = refs[-3:]
    later, second = place()
    upper = pl.program_id(0) >= half // per
    own = upper == second
    for h in range(per):
        cols = slice(h * HD, (h + 1) * HD)
        here = jnp.where(own, kept_ref[h] + low_ref[h], swapped_ref[h] + high_ref[h])
        given = jnp.where(own, gswapped_ref[h], gkept_ref[h])
        kv = jnp.where(later, here, given).astype(BF16)
        qg = jnp.where(later, given, here).astype(BF16)
        dq_ref[:, cols] = (pq_ref[:, cols].astype(F32) + scale * dot(g_ref[:, cols], kv, ((1,), (1,)))).astype(BF16)
        dk_ref[:, cols] = (pk_ref[:, cols].astype(F32) + scale * dot(v_ref[:, cols], qg, ((1,), (1,)))).astype(BF16)
        dv_ref[:, cols] = (pv_ref[:, cols].astype(F32) + scale * dot(k_ref[:, cols], qg, ((1,), (0,)))).astype(BF16)


def final(k, v, g, partials, other, states, first, size, scale, held):
    rows, width = k.shape
    half = size // 2
    per = min(half, 2)
    steps = half // per
    block = pl.BlockSpec((rows, per * HD), lambda i: (0, first // per + i))
    chunk = pl.BlockSpec((rows, per * HD), lambda i: (0, i))
    low = pl.BlockSpec((per, HD, HD), lambda i: (lax.rem(i, steps), 0, 0))
    high = pl.BlockSpec((per, HD, HD), lambda i: (steps + lax.rem(i, steps), 0, 0))
    return pl.pallas_call(
        functools.partial(final_kernel, per, half, scale),
        grid=(size // per,),
        out_shape=[jax.ShapeDtypeStruct((rows, width), BF16)] * 3,
        in_specs=[block] * 3 + [chunk] * 3 + [low, high] + [low] * 4 + [ANY] * len(held),
        out_specs=[block] * 3,
        input_output_aliases={12 + j: j for j in range(len(held))},
        compiler_params=pltpu.CompilerParams(vmem_limit_bytes=VMEM_LIMIT),
        cost_estimate=cost(6 * size * rows * HD * HD, 18 * size * rows * HD),
    )(k, v, g, *partials, other, other, *states, *held)


def local(seq, queries, keys, values, out_grad):
    rows = queries.shape[0]
    heads = queries.shape[1] // HD
    scale = float(1.0 / (HD * rows * seq) ** 0.5)
    planes = seq // 4
    at = lax.axis_index("seq")
    core_pairs = [(i, i ^ 1) for i in range(seq)]
    chip_pairs = [(i, i ^ 2) for i in range(seq)]

    def shift(value, by):
        pairs = []
        for i in range(seq):
            j = i + 4 * by if i % 2 else i - 4 * by
            pairs.append((i, j if 0 <= j < seq else i ^ 1))
        return lax.ppermute(value, "seq", pairs)

    def plane_at():
        later, _ = place()
        plane = lax.axis_index("seq") // 4
        return jnp.where(later, plane, planes - 1 - plane)

    def masked(values, steps):
        total = jnp.zeros_like(values[0])
        for value, step in zip(values, steps):
            total = total + jnp.where(plane_at() >= step, value, 0.0)
        return total

    def scan(plane, kept, partner, after):
        before, window, by = None, plane, 1
        while True:
            steps = [j * by for j in range(1, RADIX) if j * by < planes]
            arrived = [shift(window, step) for step in steps]
            by *= RADIX
            if by >= planes:
                break

            def more(window, before, *arrived):
                add = masked(arrived, steps)
                return window + add, before + add

            window, before = sums(more, 2, [window, jnp.zeros_like(plane) if before is None else before, *arrived])

        def last(kept, partner, *arrived):
            _, second = place()
            total = masked(arrived[: len(steps)], steps)
            for value in arrived[len(steps) :]:
                total = total + value
            return total + jnp.where(second, 0.0, kept), total + jnp.where(second, partner, 0.0)

        return sums(last, 2, [kept, partner, *arrived, *([] if before is None else [before])], after)

    sizes = [heads * part // sum(CHUNKS) for part in CHUNKS]
    firsts = [sum(sizes[:i]) for i in range(len(sizes))]
    first_other, *arrays = first_state((queries, keys, values, out_grad), sizes[0])
    _, keys, values, out_grad = arrays
    chunks = range(len(sizes))
    made = {}
    pieces = [()] * len(sizes)

    def wait_for(name, chunk):
        found = []
        for (c, p), after, before in PLACES:
            if before == (name, chunk):
                held = within(arrays, firsts[c], sizes[c], p * PIECE, min(PIECE, sizes[c]), scale, pieces[c], [made[after]])
                pieces[c] = held
                found.append(held[0])
        return found

    for c in chunks:
        other = other_state(arrays, firsts[c], sizes[c]) if c else first_other
        made["other", c] = lax.ppermute(other, "seq", core_pairs)
    for c in chunks:
        made["kept", c], sent = chip_state(arrays, made["other", c], firsts[c], sizes[c])
        made["partner", c] = lax.ppermute(sent, "seq", chip_pairs)
    for c in chunks:
        terms = [made["kept", c], made["partner", c]]
        (made["plane", c],) = sums(lambda a, b: (a + b,), 1, terms, wait_for("plane", c))
    done = []
    for c in chunks:
        kept, partner = made["kept", c], made["partner", c]
        back, kept_upto = scan(made["plane", c], kept, partner, wait_for("scan", c))
        swapped = lax.ppermute(back, "seq", chip_pairs)
        done.append((made["other", c], kept_upto, swapped, lax.ppermute(kept_upto, "seq", core_pairs)))

    out = ()
    for chunk, (first, size) in enumerate(zip(firsts, sizes)):
        other, kept_upto, swapped, given_kept = done[chunk]
        if out:
            swapped, out = lax.optimization_barrier((swapped, out))
        given_swapped = lax.ppermute(swapped, "seq", core_pairs)
        states = (kept_upto, swapped, given_kept, given_swapped)
        out = final(keys, values, out_grad, pieces[chunk], other, states, first, size, scale, out)
    return tuple(out)


def solution(mesh):
    spec = P(("groups", "seq"), None)
    return jax.shard_map(
        functools.partial(local, mesh.shape["seq"]),
        mesh=mesh,
        in_specs=(spec,) * 4,
        out_specs=(spec,) * 3,
        check_vma=False,
    )
```

```python
import functools

import jax
import jax.numpy as jnp
from jax import lax
from jax.experimental import pallas as pl
from jax.experimental.pallas import tpu as pltpu
from jax.sharding import PartitionSpec as P

HD = 128
CHUNKS = (8, 8)
RADIX = 2
TREE = True
PIECE = 4
PLACES = (
    ((0, 0), ("kept", 1), ("plane", 0)),
    ((0, 1), ("kept", 1), ("plane", 0)),
    ((1, 0), ("back", 0), ("scan", 1)),
    ((1, 1), ("back", 0), ("scan", 1)),
)
RADIX = 2
TREE = True
PIECE = 4
F32 = jnp.float32
BF16 = jnp.bfloat16
VMEM_LIMIT = 24 * 1024 * 1024
VMEM_MOST = 46 * 1024 * 1024
ANY = pl.BlockSpec(memory_space=pl.ANY)
HBM = pl.BlockSpec(memory_space=pltpu.HBM)
VMEM = pl.BlockSpec(memory_space=pltpu.VMEM)


def dot(a, b, dims):
    return lax.dot_general(a, b, (dims, ((), ())), preferred_element_type=F32)


def cost(flops, size):
    return pl.CostEstimate(flops=0, bytes_accessed=0, transcendentals=0)


def place():
    at = lax.axis_index("seq")
    core, chip = lax.rem(at, 2), lax.rem(at // 2, 2)
    return core == 1, core == chip


def first_kernel(size, q_ref, k_ref, v_ref, g_ref, other_ref, qv_ref, kv_ref, vv_ref, gv_ref, sem):
    later, second = place()
    width = q_ref.shape[1]
    cut = size * HD
    pieces = [(0, cut // 2), (cut // 2, cut // 2)] + ([(cut, width - cut)] if width > cut else [])

    def copies(j, source, target):
        made = []
        for n, (start, count) in enumerate(pieces):
            cols = pl.ds(start, count)
            made.append(pltpu.make_async_copy(source.at[:, cols], target.at[:, cols], sem.at[j, n]))
        return made

    q, k, v, g = (
        copies(j, source, target)
        for j, (source, target) in enumerate(((q_ref, qv_ref), (k_ref, kv_ref), (v_ref, vv_ref), (g_ref, gv_ref)))
    )

    def run(pair, refs, rest):
        for n in range(2):
            for copy in pair:
                copy[n].start()
        for copy in rest:
            for n in range(2):
                copy[n].start()
        for copy in (*rest, *pair):
            for n in range(2, len(pieces)):
                copy[n].start()
        half = size // 2
        turn = jnp.where(second, 0, half)
        for n in range(2):
            for copy in pair:
                copy[n].wait()
            for h in range(half):
                cols = slice((n * half + h) * HD, (n * half + h + 1) * HD)
                other_ref[lax.rem(n * half + turn, size) + h] = dot(refs[0][:, cols], refs[1][:, cols], ((0,), (0,)))
        for copy in rest:
            for n in range(2):
                copy[n].wait()
        for copy in (*rest, *pair):
            for n in range(2, len(pieces)):
                copy[n].wait()

    @pl.when(later)
    def _():
        run((q, g), (qv_ref, gv_ref), (k, v))

    @pl.when(jnp.logical_not(later))
    def _():
        run((k, v), (kv_ref, vv_ref), (q, g))


def first_state(arrays, size):
    rows, width = arrays[0].shape
    return pl.pallas_call(
        functools.partial(first_kernel, size),
        out_shape=[jax.ShapeDtypeStruct((size, HD, HD), F32)] + [jax.ShapeDtypeStruct((rows, width), BF16)] * 4,
        in_specs=[ANY] * 4,
        out_specs=[VMEM] * 5,
        scratch_shapes=[pltpu.SemaphoreType.DMA((4, 3))],
        compiler_params=pltpu.CompilerParams(vmem_limit_bytes=VMEM_MOST),
        cost_estimate=cost(2 * size * rows * HD * HD, 16 * rows * width),
    )(*arrays)


def other_kernel(first, size, q_ref, k_ref, v_ref, g_ref, out_ref):
    later, second = place()
    half = size // 2
    turn = jnp.where(second, 0, half)

    def run(a_ref, b_ref):
        for h in range(size):
            cols = slice((first + h) * HD, (first + h + 1) * HD)
            at = lax.rem(h // half * half + turn, size) + h % half
            out_ref[at] = dot(a_ref[:, cols], b_ref[:, cols], ((0,), (0,)))

    @pl.when(later)
    def _():
        run(q_ref, g_ref)

    @pl.when(jnp.logical_not(later))
    def _():
        run(k_ref, v_ref)


def mine_kernel(first, size, q_ref, k_ref, v_ref, g_ref, other_ref, kept_ref, sent_ref):
    later, second = place()
    half = size // 2

    def run(pair, swap):
        refs = (sent_ref, kept_ref) if swap else (kept_ref, sent_ref)
        for h in range(size):
            cols = slice((first + h) * HD, (first + h + 1) * HD)
            at = (h + (half if swap else 0)) % size
            value = dot(pair[0][:, cols], pair[1][:, cols], ((0,), (0,)))
            refs[h // half][h % half] = value + other_ref[at]

    for is_later, pair in ((True, (k_ref, v_ref)), (False, (q_ref, g_ref))):
        for swap in (True, False):
            pl.when(jnp.logical_and(later == is_later, second == swap))(functools.partial(run, pair, swap))


def other_state(arrays, first, size):
    rows = arrays[0].shape[0]
    return pl.pallas_call(
        functools.partial(other_kernel, first, size),
        out_shape=jax.ShapeDtypeStruct((size, HD, HD), F32),
        in_specs=[VMEM] * 4,
        out_specs=VMEM,
        compiler_params=pltpu.CompilerParams(vmem_limit_bytes=VMEM_LIMIT),
        cost_estimate=cost(2 * size * rows * HD * HD, 4 * size * rows * HD),
    )(*arrays)


def chip_state(arrays, other, first, size):
    rows = arrays[0].shape[0]
    half = jax.ShapeDtypeStruct((size // 2, HD, HD), F32)
    return pl.pallas_call(
        functools.partial(mine_kernel, first, size),
        out_shape=[half, half],
        in_specs=[VMEM] * 5,
        out_specs=[VMEM, VMEM],
        compiler_params=pltpu.CompilerParams(vmem_limit_bytes=VMEM_LIMIT),
        cost_estimate=cost(2 * size * rows * HD * HD, 4 * size * rows * HD),
    )(*arrays, other)


def sums_kernel(count, outs, work, *refs):
    values = work(*[ref[...] for ref in refs[:count]])
    for ref, value in zip(refs[-outs:], values):
        ref[...] = value


def sums(work, outs, values, after=()):
    return pl.pallas_call(
        functools.partial(sums_kernel, len(values), outs, work),
        out_shape=[jax.ShapeDtypeStruct(values[0].shape, F32)] * outs,
        in_specs=[VMEM] * len(values) + [ANY] * len(after),
        out_specs=[VMEM] * outs,
        compiler_params=pltpu.CompilerParams(vmem_limit_bytes=VMEM_LIMIT),
        cost_estimate=cost(values[0].size, 8 * values[0].size),
    )(*values, *after)


def within_kernel(heads, scale, q_ref, k_ref, v_ref, g_ref, *refs):
    dq_ref, dk_ref, dv_ref = refs[-3:]
    rows = q_ref.shape[0]
    at = lax.broadcasted_iota(jnp.int32, (rows, rows), 0)
    upto = lax.broadcasted_iota(jnp.int32, (rows, rows), 1) <= at
    for h in range(heads):
        cols = slice(h * HD, (h + 1) * HD)
        q, k, v, g = q_ref[:, cols], k_ref[:, cols], v_ref[:, cols], g_ref[:, cols]
        weights = jnp.where(upto, dot(q, k, ((1,), (1,))) * scale, 0.0).astype(BF16)
        scores = jnp.where(upto, dot(g, v, ((1,), (1,))) * scale, 0.0).astype(BF16)
        dq_ref[:, cols] = dot(scores, k, ((1,), (0,))).astype(BF16)
        dk_ref[:, cols] = dot(scores, q, ((0,), (0,))).astype(BF16)
        dv_ref[:, cols] = dot(weights, g, ((0,), (0,))).astype(BF16)


def within(arrays, first, size, start, heads, scale, held, after):
    rows = arrays[0].shape[0]
    per = min(heads, 2)
    block = pl.BlockSpec((rows, per * HD), lambda i: (0, (first + start) // per + i))
    out = pl.BlockSpec((rows, per * HD), lambda i: (0, start // per + i))
    return pl.pallas_call(
        functools.partial(within_kernel, per, scale),
        grid=(heads // per,),
        out_shape=[jax.ShapeDtypeStruct((rows, size * HD), BF16)] * 3,
        in_specs=[block] * 4 + [ANY] * len((*held, *after)),
        out_specs=[out] * 3,
        input_output_aliases={4 + j: j for j in range(len(held))},
        compiler_params=pltpu.CompilerParams(vmem_limit_bytes=VMEM_LIMIT),
        cost_estimate=cost(heads * rows * HD, heads * rows * HD),
    )(*arrays, *held, *after)


def final_kernel(per, half, scale, *refs):
    k_ref, v_ref, g_ref, pq_ref, pk_ref, pv_ref = refs[:6]
    low_ref, high_ref, kept_ref, swapped_ref, gkept_ref, gswapped_ref = refs[6:12]
    dq_ref, dk_ref, dv_ref = refs[-3:]
    later, second = place()
    upper = pl.program_id(0) >= half // per
    own = upper == second
    for h in range(per):
        cols = slice(h * HD, (h + 1) * HD)
        here = jnp.where(own, kept_ref[h] + low_ref[h], swapped_ref[h] + high_ref[h])
        given = jnp.where(own, gswapped_ref[h], gkept_ref[h])
        kv = jnp.where(later, here, given).astype(BF16)
        qg = jnp.where(later, given, here).astype(BF16)
        dq_ref[:, cols] = (pq_ref[:, cols].astype(F32) + scale * dot(g_ref[:, cols], kv, ((1,), (1,)))).astype(BF16)
        dk_ref[:, cols] = (pk_ref[:, cols].astype(F32) + scale * dot(v_ref[:, cols], qg, ((1,), (1,)))).astype(BF16)
        dv_ref[:, cols] = (pv_ref[:, cols].astype(F32) + scale * dot(k_ref[:, cols], qg, ((1,), (0,)))).astype(BF16)


def final(k, v, g, partials, other, states, first, size, scale, held):
    rows, width = k.shape
    half = size // 2
    per = min(half, 2)
    steps = half // per
    block = pl.BlockSpec((rows, per * HD), lambda i: (0, first // per + i))
    chunk = pl.BlockSpec((rows, per * HD), lambda i: (0, i))
    low = pl.BlockSpec((per, HD, HD), lambda i: (lax.rem(i, steps), 0, 0))
    high = pl.BlockSpec((per, HD, HD), lambda i: (steps + lax.rem(i, steps), 0, 0))
    return pl.pallas_call(
        functools.partial(final_kernel, per, half, scale),
        grid=(size // per,),
        out_shape=[jax.ShapeDtypeStruct((rows, width), BF16)] * 3,
        in_specs=[block] * 3 + [chunk] * 3 + [low, high] + [low] * 4 + [ANY] * len(held),
        out_specs=[block] * 3,
        input_output_aliases={12 + j: j for j in range(len(held))},
        compiler_params=pltpu.CompilerParams(vmem_limit_bytes=VMEM_LIMIT),
        cost_estimate=cost(6 * size * rows * HD * HD, 18 * size * rows * HD),
    )(k, v, g, *partials, other, other, *states, *held)


def local(seq, queries, keys, values, out_grad):
    rows = queries.shape[0]
    heads = queries.shape[1] // HD
    scale = float(1.0 / (HD * rows * seq) ** 0.5)
    planes = seq // 4
    core_pairs = [(i, i ^ 1) for i in range(seq)]
    chip_pairs = [(i, i ^ 2) for i in range(seq)]

    def moved(value, plan):
        pairs = {}
        for to, source in plan.items():
            for chip in range(2):
                pairs[4 * source + 2 * chip + 1] = 4 * to + 2 * chip + 1
                pairs[4 * (planes - 1 - source) + 2 * chip] = 4 * (planes - 1 - to) + 2 * chip
        free = set(range(seq)) - set(pairs.values())
        for i in range(seq):
            if i not in pairs and i ^ 1 in free:
                pairs[i] = i ^ 1
                free.discard(i ^ 1)
        for chip in range(2):
            senders = [i for i in range(seq) if i not in pairs and i // 2 % 2 == chip]
            targets = [i for i in sorted(free) if i // 2 % 2 == chip]
            pairs.update(zip(senders, targets))
        return lax.ppermute(value, "seq", sorted(pairs.items()))

    def masked(total, values, plans):
        later, _ = place()
        plane = lax.axis_index("seq") // 4
        plane = jnp.where(later, plane, planes - 1 - plane)
        for value, plan in zip(values, plans):
            wanted = functools.reduce(jnp.logical_or, [plane == to for to in plan])
            total = total + jnp.where(wanted, value, 0.0)
        return total

    if planes == 4 and TREE:
        levels = [[{1: 0, 3: 2}], [{2: 1}, {3: 1}]]
    else:
        levels, by = [], 1
        while by < planes:
            levels.append([{to: to - j * by for to in range(j * by, planes)} for j in range(1, RADIX) if j * by < planes])
            by *= RADIX

    sizes = [heads * part // sum(CHUNKS) for part in CHUNKS]
    firsts = [sum(sizes[:i]) for i in range(len(sizes))]
    first_other, *arrays = first_state((queries, keys, values, out_grad), sizes[0])
    _, keys, values, out_grad = arrays
    chunks = range(len(sizes))
    made = {}
    pieces = [()] * len(sizes)

    def wait_for(name, chunk):
        found = []
        for (c, p), after, before in PLACES:
            if before == (name, chunk):
                held = within(arrays, firsts[c], sizes[c], p * PIECE, min(PIECE, sizes[c]), scale, pieces[c], [made[after]])
                pieces[c] = held
                found.append(held[0])
        return found

    for c in chunks:
        other = other_state(arrays, firsts[c], sizes[c]) if c else first_other
        made["other", c] = lax.ppermute(other, "seq", core_pairs)
    for c in chunks:
        made["kept", c], sent = chip_state(arrays, made["other", c], firsts[c], sizes[c])
        made["partner", c] = lax.ppermute(sent, "seq", chip_pairs)
    def stage(name, c, before):
        return wait_for(name, c) + ([made[before, c + 1]] if c + 1 < len(sizes) else [])

    for c in chunks:
        terms = [made["kept", c], made["partner", c]]
        (made["plane", c],) = sums(lambda a, b: (a + b,), 1, terms, stage("plane", c, "kept"))
        made["before", c] = None
    last = "plane"
    for number, plans in enumerate(levels[:-1]):
        name = f"window{number}"
        for c in chunks:

            def more(window, *arrived):
                add = masked(jnp.zeros_like(window), arrived[: len(plans)], plans)
                return window + add, sum(arrived[len(plans) :], add)

            window = made[last, c]
            arrived = [moved(window, plan) for plan in plans]
            held = [] if made["before", c] is None else [made["before", c]]
            made[name, c], made["before", c] = sums(more, 2, [window, *arrived, *held], stage(name, c, last))
        last = name

    done = []
    for c in chunks:
        plans = levels[-1]

        def ready(kept, partner, *arrived):
            _, second = place()
            total = masked(jnp.zeros_like(kept), arrived[: len(plans)], plans)
            total = sum(arrived[len(plans) :], total)
            return total + jnp.where(second, 0.0, kept), total + jnp.where(second, partner, 0.0)

        arrived = [moved(made[last, c], plan) for plan in plans]
        held = [] if made["before", c] is None else [made["before", c]]
        terms = [made["kept", c], made["partner", c], *arrived, *held]
        made["back", c], kept_upto = sums(ready, 2, terms, stage("scan", c, last))
        swapped = lax.ppermute(made["back", c], "seq", chip_pairs)
        done.append((made["other", c], kept_upto, swapped, lax.ppermute(kept_upto, "seq", core_pairs)))

    out = ()
    for chunk, (first, size) in enumerate(zip(firsts, sizes)):
        other, kept_upto, swapped, given_kept = done[chunk]
        ahead = [made["back", chunk + 1]] if chunk + 1 < len(sizes) else []
        swapped, out, ahead = lax.optimization_barrier((swapped, out, ahead))
        given_swapped = lax.ppermute(swapped, "seq", core_pairs)
        states = (kept_upto, swapped, given_kept, given_swapped)
        out = final(keys, values, out_grad, pieces[chunk], other, states, first, size, scale, out)
    return tuple(out)


def solution(mesh):
    spec = P(("groups", "seq"), None)
    return jax.shard_map(
        functools.partial(local, mesh.shape["seq"]),
        mesh=mesh,
        in_specs=(spec,) * 4,
        out_specs=(spec,) * 3,
        check_vma=False,
    )
```

```python
import functools

import jax
import jax.numpy as jnp
from jax import lax
from jax.experimental import pallas as pl
from jax.experimental.pallas import tpu as pltpu
from jax.sharding import PartitionSpec as P

HD = 128
CHUNKS = (8, 8)
RADIX = 2
TREE = True
PIECE = 4
PLACES = (
    ((0, 0), ("kept", 1), ("plane", 0)),
    ((0, 1), ("kept", 1), ("plane", 0)),
    ((1, 0), ("back", 0), ("scan", 1)),
    ((1, 1), ("back", 0), ("scan", 1)),
)
F32 = jnp.float32
BF16 = jnp.bfloat16
VMEM_LIMIT = 24 * 1024 * 1024
VMEM_MOST = 46 * 1024 * 1024
ANY = pl.BlockSpec(memory_space=pl.ANY)
HBM = pl.BlockSpec(memory_space=pltpu.HBM)
VMEM = pl.BlockSpec(memory_space=pltpu.VMEM)


def dot(a, b, dims):
    return lax.dot_general(a, b, (dims, ((), ())), preferred_element_type=F32)


def cost(flops, size):
    return pl.CostEstimate(flops=0, bytes_accessed=0, transcendentals=0)


def place():
    at = lax.axis_index("seq")
    core, chip = lax.rem(at, 2), lax.rem(at // 2, 2)
    return core == 1, core == chip


def first_kernel(size, q_ref, k_ref, v_ref, g_ref, other_ref, qv_ref, kv_ref, vv_ref, gv_ref, sem):
    later, second = place()
    width = q_ref.shape[1]
    cut = size * HD
    pieces = [(0, cut // 2), (cut // 2, cut // 2)] + ([(cut, width - cut)] if width > cut else [])

    def copies(j, source, target):
        made = []
        for n, (start, count) in enumerate(pieces):
            cols = pl.ds(start, count)
            made.append(pltpu.make_async_copy(source.at[:, cols], target.at[:, cols], sem.at[j, n]))
        return made

    q, k, v, g = (
        copies(j, source, target)
        for j, (source, target) in enumerate(((q_ref, qv_ref), (k_ref, kv_ref), (v_ref, vv_ref), (g_ref, gv_ref)))
    )

    def run(pair, refs, rest):
        for n in range(2):
            for copy in pair:
                copy[n].start()
        for copy in rest:
            for n in range(2):
                copy[n].start()
        for copy in (*rest, *pair):
            for n in range(2, len(pieces)):
                copy[n].start()
        half = size // 2
        turn = jnp.where(second, 0, half)
        for n in range(2):
            for copy in pair:
                copy[n].wait()
            for h in range(half):
                cols = slice((n * half + h) * HD, (n * half + h + 1) * HD)
                other_ref[lax.rem(n * half + turn, size) + h] = dot(refs[0][:, cols], refs[1][:, cols], ((0,), (0,)))
        for copy in rest:
            for n in range(2):
                copy[n].wait()
        for copy in (*rest, *pair):
            for n in range(2, len(pieces)):
                copy[n].wait()

    @pl.when(later)
    def _():
        run((q, g), (qv_ref, gv_ref), (k, v))

    @pl.when(jnp.logical_not(later))
    def _():
        run((k, v), (kv_ref, vv_ref), (q, g))


def first_state(arrays, size):
    rows, width = arrays[0].shape
    return pl.pallas_call(
        functools.partial(first_kernel, size),
        out_shape=[jax.ShapeDtypeStruct((size, HD, HD), F32)] + [jax.ShapeDtypeStruct((rows, width), BF16)] * 4,
        in_specs=[ANY] * 4,
        out_specs=[VMEM] * 5,
        scratch_shapes=[pltpu.SemaphoreType.DMA((4, 3))],
        compiler_params=pltpu.CompilerParams(vmem_limit_bytes=VMEM_MOST),
        cost_estimate=cost(2 * size * rows * HD * HD, 16 * rows * width),
    )(*arrays)


def other_kernel(first, size, q_ref, k_ref, v_ref, g_ref, out_ref):
    later, second = place()
    half = size // 2
    turn = jnp.where(second, 0, half)

    def run(a_ref, b_ref):
        for h in range(size):
            cols = slice((first + h) * HD, (first + h + 1) * HD)
            at = lax.rem(h // half * half + turn, size) + h % half
            out_ref[at] = dot(a_ref[:, cols], b_ref[:, cols], ((0,), (0,)))

    @pl.when(later)
    def _():
        run(q_ref, g_ref)

    @pl.when(jnp.logical_not(later))
    def _():
        run(k_ref, v_ref)


def mine_kernel(first, size, q_ref, k_ref, v_ref, g_ref, other_ref, kept_ref, sent_ref):
    later, second = place()
    half = size // 2

    def run(pair, swap):
        refs = (sent_ref, kept_ref) if swap else (kept_ref, sent_ref)
        for h in range(size):
            cols = slice((first + h) * HD, (first + h + 1) * HD)
            at = (h + (half if swap else 0)) % size
            value = dot(pair[0][:, cols], pair[1][:, cols], ((0,), (0,)))
            refs[h // half][h % half] = value + other_ref[at]

    for is_later, pair in ((True, (k_ref, v_ref)), (False, (q_ref, g_ref))):
        for swap in (True, False):
            pl.when(jnp.logical_and(later == is_later, second == swap))(functools.partial(run, pair, swap))


def other_state(arrays, first, size):
    rows = arrays[0].shape[0]
    return pl.pallas_call(
        functools.partial(other_kernel, first, size),
        out_shape=jax.ShapeDtypeStruct((size, HD, HD), F32),
        in_specs=[VMEM] * 4,
        out_specs=VMEM,
        compiler_params=pltpu.CompilerParams(vmem_limit_bytes=VMEM_LIMIT),
        cost_estimate=cost(2 * size * rows * HD * HD, 4 * size * rows * HD),
    )(*arrays)


def chip_state(arrays, other, first, size):
    rows = arrays[0].shape[0]
    half = jax.ShapeDtypeStruct((size // 2, HD, HD), F32)
    return pl.pallas_call(
        functools.partial(mine_kernel, first, size),
        out_shape=[half, half],
        in_specs=[VMEM] * 5,
        out_specs=[VMEM, VMEM],
        compiler_params=pltpu.CompilerParams(vmem_limit_bytes=VMEM_LIMIT),
        cost_estimate=cost(2 * size * rows * HD * HD, 4 * size * rows * HD),
    )(*arrays, other)


def sums_kernel(count, outs, work, *refs):
    values = work(*[ref[...] for ref in refs[:count]])
    for ref, value in zip(refs[-outs:], values):
        ref[...] = value


def sums(work, outs, values, after=()):
    return pl.pallas_call(
        functools.partial(sums_kernel, len(values), outs, work),
        out_shape=[jax.ShapeDtypeStruct(values[0].shape, F32)] * outs,
        in_specs=[VMEM] * len(values) + [ANY] * len(after),
        out_specs=[VMEM] * outs,
        compiler_params=pltpu.CompilerParams(vmem_limit_bytes=VMEM_LIMIT),
        cost_estimate=cost(values[0].size, 8 * values[0].size),
    )(*values, *after)


def within_kernel(first, heads, scale, q_ref, k_ref, v_ref, g_ref, *refs):
    dq_ref, dk_ref, dv_ref = refs[-3:]
    rows = q_ref.shape[0]
    cut = 256 if rows > 256 else rows

    def causal(a, b, low):
        at = low + lax.broadcasted_iota(jnp.int32, (a.shape[0], b.shape[0]), 0)
        upto = lax.broadcasted_iota(jnp.int32, (a.shape[0], b.shape[0]), 1) <= at
        return jnp.where(upto, dot(a, b, ((1,), (1,))) * scale, 0.0).astype(BF16)

    for h in range(heads):
        cols = slice(h * HD, (h + 1) * HD)
        whole = slice((first + h) * HD, (first + h + 1) * HD)
        q, k, v, g = q_ref[:, whole], k_ref[:, whole], v_ref[:, whole], g_ref[:, whole]
        weights = causal(q[:cut], k[:cut], 0)
        scores = causal(g[:cut], v[:cut], 0)
        dq_ref[:cut, cols] = dot(scores, k[:cut], ((1,), (0,))).astype(BF16)
        dk = dot(scores, q[:cut], ((0,), (0,)))
        dv = dot(weights, g[:cut], ((0,), (0,)))
        if cut < rows:
            weights = causal(q[cut:], k, cut)
            scores = causal(g[cut:], v, cut)
            dq_ref[cut:, cols] = dot(scores, k, ((1,), (0,))).astype(BF16)
            low = dot(scores, q[cut:], ((0,), (0,)))
            dk, dk_ref[cut:, cols] = dk + low[:cut], low[cut:].astype(BF16)
            low = dot(weights, g[cut:], ((0,), (0,)))
            dv, dv_ref[cut:, cols] = dv + low[:cut], low[cut:].astype(BF16)
        dk_ref[:cut, cols] = dk.astype(BF16)
        dv_ref[:cut, cols] = dv.astype(BF16)


def within(arrays, first, heads, scale, after):
    rows = arrays[0].shape[0]
    return pl.pallas_call(
        functools.partial(within_kernel, first, heads, scale),
        out_shape=[jax.ShapeDtypeStruct((rows, heads * HD), BF16)] * 3,
        in_specs=[VMEM] * 4 + [ANY] * len(after),
        out_specs=[VMEM] * 3,
        compiler_params=pltpu.CompilerParams(vmem_limit_bytes=VMEM_LIMIT),
        cost_estimate=cost(heads * rows * HD, heads * rows * HD),
    )(*arrays, *after)


def diagonal(blocks):
    count = len(blocks)
    rows = [jnp.concatenate([b if j == i else jnp.zeros_like(b) for j in range(count)], axis=1) for i, b in enumerate(blocks)]
    return jnp.concatenate(rows, axis=0)


def final_kernel(first, half, scale, *refs):
    k_ref, v_ref, g_ref, other_ref, kept_ref, swapped_ref, gkept_ref, gswapped_ref = refs[:8]
    parts = refs[8:]
    piece = min(PIECE, 2 * half)
    buffers, sem, outs = refs[-4:-1], refs[-1], refs[-7:-4]
    later, second = place()
    per = 2 if half % 2 == 0 else 1
    copies = []
    for n in range(2 * half // per):
        upper = n * per >= half
        own = second if upper else jnp.logical_not(second)
        kv, qg = [], []
        for h in range(per):
            at = n * per % half + h
            here = jnp.where(own, kept_ref[at] + other_ref[at], swapped_ref[at] + other_ref[half + at])
            given = jnp.where(own, gswapped_ref[at], gkept_ref[at])
            kv.append(jnp.where(later, here, given).astype(BF16))
            qg.append(jnp.where(later, given, here).astype(BF16))
        kv, qg = diagonal(kv), diagonal(qg)
        cols = slice(n * per * HD, (n + 1) * per * HD)
        whole = slice((first + n * per) * HD, (first + (n + 1) * per) * HD)
        terms = (
            dot(g_ref[:, whole], kv, ((1,), (1,))),
            dot(v_ref[:, whole], qg, ((1,), (1,))),
            dot(k_ref[:, whole], qg, ((1,), (0,))),
        )
        held = slice(n * per % piece * HD, (n * per % piece + per) * HD)
        for j, term in enumerate(terms):
            part = parts[n * per // piece * 3 + j][:, held]
            buffers[j][:, cols] = (part.astype(F32) + scale * term).astype(BF16)
            copies.append(pltpu.make_async_copy(buffers[j].at[:, cols], outs[j].at[:, whole], sem.at[n, j]))
            copies[-1].start()
    for copy in copies:
        copy.wait()


def final(k, v, g, partials, other, states, first, size, scale, held):
    rows, width = k.shape
    return pl.pallas_call(
        functools.partial(final_kernel, first, size // 2, scale),
        out_shape=[jax.ShapeDtypeStruct((rows, width), BF16)] * 3,
        in_specs=[VMEM] * (8 + len(partials)) + [ANY] * len(held),
        out_specs=[ANY] * 3,
        scratch_shapes=[pltpu.VMEM((rows, size * HD), BF16)] * 3 + [pltpu.SemaphoreType.DMA((size, 3))],
        input_output_aliases={8 + len(partials) + j: j for j in range(len(held))},
        compiler_params=pltpu.CompilerParams(vmem_limit_bytes=VMEM_LIMIT),
        cost_estimate=cost(6 * size * rows * HD * HD, 18 * size * rows * HD),
    )(k, v, g, other, *states, *partials, *held)


def local(seq, queries, keys, values, out_grad):
    rows = queries.shape[0]
    heads = queries.shape[1] // HD
    scale = float(1.0 / (HD * rows * seq) ** 0.5)
    planes = seq // 4
    core_pairs = [(i, i ^ 1) for i in range(seq)]
    chip_pairs = [(i, i ^ 2) for i in range(seq)]

    def moved(value, plan):
        pairs = {}
        for to, source in plan.items():
            for chip in range(2):
                pairs[4 * source + 2 * chip + 1] = 4 * to + 2 * chip + 1
                pairs[4 * (planes - 1 - source) + 2 * chip] = 4 * (planes - 1 - to) + 2 * chip
        free = set(range(seq)) - set(pairs.values())
        for i in range(seq):
            if i not in pairs and i ^ 1 in free:
                pairs[i] = i ^ 1
                free.discard(i ^ 1)
        for chip in range(2):
            senders = [i for i in range(seq) if i not in pairs and i // 2 % 2 == chip]
            targets = [i for i in sorted(free) if i // 2 % 2 == chip]
            pairs.update(zip(senders, targets))
        return lax.ppermute(value, "seq", sorted(pairs.items()))

    def masked(total, values, plans):
        later, _ = place()
        plane = lax.axis_index("seq") // 4
        plane = jnp.where(later, plane, planes - 1 - plane)
        for value, plan in zip(values, plans):
            wanted = functools.reduce(jnp.logical_or, [plane == to for to in plan])
            total = total + jnp.where(wanted, value, 0.0)
        return total

    if planes == 4 and TREE:
        levels = [[{1: 0, 3: 2}], [{2: 1}, {3: 1}]]
    else:
        levels, by = [], 1
        while by < planes:
            levels.append([{to: to - j * by for to in range(j * by, planes)} for j in range(1, RADIX) if j * by < planes])
            by *= RADIX

    sizes = [heads * part // sum(CHUNKS) for part in CHUNKS]
    firsts = [sum(sizes[:i]) for i in range(len(sizes))]
    first_other, *arrays = first_state((queries, keys, values, out_grad), sizes[0])
    _, keys, values, out_grad = arrays
    chunks = range(len(sizes))
    made = {}
    pieces = [[] for _ in sizes]

    def wait_for(name, chunk):
        found = []
        for (c, p), after, before in PLACES:
            if before == (name, chunk):
                part = within(arrays, firsts[c] + p * PIECE, min(PIECE, sizes[c]), scale, [made[after]])
                pieces[c] = [*pieces[c], *part]
                found.append(part[0])
        return found

    for c in chunks:
        other = other_state(arrays, firsts[c], sizes[c]) if c else first_other
        made["other", c] = lax.ppermute(other, "seq", core_pairs)
    for c in chunks:
        made["kept", c], sent = chip_state(arrays, made["other", c], firsts[c], sizes[c])
        made["partner", c] = lax.ppermute(sent, "seq", chip_pairs)
    def stage(name, c, before):
        return wait_for(name, c) + ([made[before, c + 1]] if c + 1 < len(sizes) else [])

    for c in chunks:
        terms = [made["kept", c], made["partner", c]]
        (made["plane", c],) = sums(lambda a, b: (a + b,), 1, terms, stage("plane", c, "kept"))
        made["before", c] = None
    last = "plane"
    for number, plans in enumerate(levels[:-1]):
        name = f"window{number}"
        for c in chunks:

            def more(window, *arrived):
                add = masked(jnp.zeros_like(window), arrived[: len(plans)], plans)
                return window + add, sum(arrived[len(plans) :], add)

            window = made[last, c]
            arrived = [moved(window, plan) for plan in plans]
            held = [] if made["before", c] is None else [made["before", c]]
            made[name, c], made["before", c] = sums(more, 2, [window, *arrived, *held], stage(name, c, last))
        last = name

    done = []
    for c in chunks:
        plans = levels[-1]

        def ready(kept, partner, *arrived):
            _, second = place()
            total = masked(jnp.zeros_like(kept), arrived[: len(plans)], plans)
            total = sum(arrived[len(plans) :], total)
            return total + jnp.where(second, 0.0, kept), total + jnp.where(second, partner, 0.0)

        arrived = [moved(made[last, c], plan) for plan in plans]
        held = [] if made["before", c] is None else [made["before", c]]
        terms = [made["kept", c], made["partner", c], *arrived, *held]
        made["back", c], kept_upto = sums(ready, 2, terms, stage("scan", c, last))
        swapped = lax.ppermute(made["back", c], "seq", chip_pairs)
        done.append((made["other", c], kept_upto, swapped, lax.ppermute(kept_upto, "seq", core_pairs)))

    out = ()
    for chunk, (first, size) in enumerate(zip(firsts, sizes)):
        other, kept_upto, swapped, given_kept = done[chunk]
        ahead = [made["back", chunk + 1]] if chunk + 1 < len(sizes) else []
        swapped, out, ahead = lax.optimization_barrier((swapped, out, ahead))
        given_swapped = lax.ppermute(swapped, "seq", core_pairs)
        states = (kept_upto, swapped, given_kept, given_swapped)
        out = final(keys, values, out_grad, pieces[chunk], other, states, first, size, scale, out)
    return tuple(out)


def solution(mesh):
    spec = P(("groups", "seq"), None)
    return jax.shard_map(
        functools.partial(local, mesh.shape["seq"]),
        mesh=mesh,
        in_specs=(spec,) * 4,
        out_specs=(spec,) * 3,
        check_vma=False,
    )
```

```python
import functools

import jax
import jax.numpy as jnp
from jax import lax
from jax.experimental import pallas as pl
from jax.experimental.pallas import tpu as pltpu
from jax.sharding import PartitionSpec as P

HD = 128
CHUNKS = (8, 8)
RADIX = 2
TREE = True
PIECE = 4
PLACES = (
    ((0, 0), ("kept", 1), ("plane", 0)),
    ((0, 1), ("kept", 1), ("plane", 0)),
    ((1, 0), ("back", 0), ("scan", 1)),
    ((1, 1), ("back", 0), ("scan", 1)),
)
F32 = jnp.float32
BF16 = jnp.bfloat16
VMEM_LIMIT = 24 * 1024 * 1024
VMEM_MOST = 46 * 1024 * 1024
ANY = pl.BlockSpec(memory_space=pl.ANY)
HBM = pl.BlockSpec(memory_space=pltpu.HBM)
VMEM = pl.BlockSpec(memory_space=pltpu.VMEM)


def dot(a, b, dims):
    return lax.dot_general(a, b, (dims, ((), ())), preferred_element_type=F32)


def cost(flops, size):
    return pl.CostEstimate(flops=0, bytes_accessed=0, transcendentals=0)


def place():
    at = lax.axis_index("seq")
    core, chip = lax.rem(at, 2), lax.rem(at // 2, 2)
    return core == 1, core == chip


def first_kernel(size, q_ref, k_ref, v_ref, g_ref, other_ref, qv_ref, kv_ref, vv_ref, gv_ref, sem):
    later, second = place()
    width = q_ref.shape[1]
    cut = size * HD
    pieces = [(0, cut // 2), (cut // 2, cut // 2)] + ([(cut, width - cut)] if width > cut else [])

    def copies(j, source, target):
        made = []
        for n, (start, count) in enumerate(pieces):
            cols = pl.ds(start, count)
            made.append(pltpu.make_async_copy(source.at[:, cols], target.at[:, cols], sem.at[j, n]))
        return made

    q, k, v, g = (
        copies(j, source, target)
        for j, (source, target) in enumerate(((q_ref, qv_ref), (k_ref, kv_ref), (v_ref, vv_ref), (g_ref, gv_ref)))
    )

    def run(pair, refs, rest):
        for n in range(2):
            for copy in pair:
                copy[n].start()
        for copy in rest:
            for n in range(2):
                copy[n].start()
        for copy in (*rest, *pair):
            for n in range(2, len(pieces)):
                copy[n].start()
        half = size // 2
        turn = jnp.where(second, 0, half)
        for n in range(2):
            for copy in pair:
                copy[n].wait()
            for h in range(half):
                cols = slice((n * half + h) * HD, (n * half + h + 1) * HD)
                other_ref[lax.rem(n * half + turn, size) + h] = dot(refs[0][:, cols], refs[1][:, cols], ((0,), (0,)))
        for copy in rest:
            for n in range(2):
                copy[n].wait()
        for copy in (*rest, *pair):
            for n in range(2, len(pieces)):
                copy[n].wait()

    @pl.when(later)
    def _():
        run((q, g), (qv_ref, gv_ref), (k, v))

    @pl.when(jnp.logical_not(later))
    def _():
        run((k, v), (kv_ref, vv_ref), (q, g))


def first_state(arrays, size):
    rows, width = arrays[0].shape
    return pl.pallas_call(
        functools.partial(first_kernel, size),
        out_shape=[jax.ShapeDtypeStruct((size, HD, HD), F32)] + [jax.ShapeDtypeStruct((rows, width), BF16)] * 4,
        in_specs=[ANY] * 4,
        out_specs=[VMEM] * 5,
        scratch_shapes=[pltpu.SemaphoreType.DMA((4, 3))],
        compiler_params=pltpu.CompilerParams(vmem_limit_bytes=VMEM_MOST),
        cost_estimate=cost(2 * size * rows * HD * HD, 16 * rows * width),
    )(*arrays)


def other_kernel(first, size, q_ref, k_ref, v_ref, g_ref, out_ref):
    later, second = place()
    half = size // 2
    turn = jnp.where(second, 0, half)

    def run(a_ref, b_ref):
        for h in range(size):
            cols = slice((first + h) * HD, (first + h + 1) * HD)
            at = lax.rem(h // half * half + turn, size) + h % half
            out_ref[at] = dot(a_ref[:, cols], b_ref[:, cols], ((0,), (0,)))

    @pl.when(later)
    def _():
        run(q_ref, g_ref)

    @pl.when(jnp.logical_not(later))
    def _():
        run(k_ref, v_ref)


def mine_kernel(first, size, q_ref, k_ref, v_ref, g_ref, other_ref, kept_ref, sent_ref):
    later, second = place()
    half = size // 2

    def run(pair, swap):
        refs = (sent_ref, kept_ref) if swap else (kept_ref, sent_ref)
        for h in range(size):
            cols = slice((first + h) * HD, (first + h + 1) * HD)
            at = (h + (half if swap else 0)) % size
            value = dot(pair[0][:, cols], pair[1][:, cols], ((0,), (0,)))
            refs[h // half][h % half] = value + other_ref[at]

    for is_later, pair in ((True, (k_ref, v_ref)), (False, (q_ref, g_ref))):
        for swap in (True, False):
            pl.when(jnp.logical_and(later == is_later, second == swap))(functools.partial(run, pair, swap))


def other_state(arrays, first, size):
    rows = arrays[0].shape[0]
    return pl.pallas_call(
        functools.partial(other_kernel, first, size),
        out_shape=jax.ShapeDtypeStruct((size, HD, HD), F32),
        in_specs=[VMEM] * 4,
        out_specs=VMEM,
        compiler_params=pltpu.CompilerParams(vmem_limit_bytes=VMEM_LIMIT),
        cost_estimate=cost(2 * size * rows * HD * HD, 4 * size * rows * HD),
    )(*arrays)


def chip_state(arrays, other, first, size):
    rows = arrays[0].shape[0]
    half = jax.ShapeDtypeStruct((size // 2, HD, HD), F32)
    return pl.pallas_call(
        functools.partial(mine_kernel, first, size),
        out_shape=[half, half],
        in_specs=[VMEM] * 5,
        out_specs=[VMEM, VMEM],
        compiler_params=pltpu.CompilerParams(vmem_limit_bytes=VMEM_LIMIT),
        cost_estimate=cost(2 * size * rows * HD * HD, 4 * size * rows * HD),
    )(*arrays, other)


def sums_kernel(count, outs, work, *refs):
    values = work(*[ref[...] for ref in refs[:count]])
    for ref, value in zip(refs[-outs:], values):
        ref[...] = value


def sums(work, outs, values, after=()):
    return pl.pallas_call(
        functools.partial(sums_kernel, len(values), outs, work),
        out_shape=[jax.ShapeDtypeStruct(values[0].shape, F32)] * outs,
        in_specs=[VMEM] * len(values) + [ANY] * len(after),
        out_specs=[VMEM] * outs,
        compiler_params=pltpu.CompilerParams(vmem_limit_bytes=VMEM_LIMIT),
        cost_estimate=cost(values[0].size, 8 * values[0].size),
    )(*values, *after)


def within_kernel(first, heads, scale, q_ref, k_ref, v_ref, g_ref, *refs):
    dq_ref, dk_ref, dv_ref = refs[-3:]
    rows = q_ref.shape[0]
    cut = 256 if rows > 256 else rows

    def causal(a, b, low):
        at = low + lax.broadcasted_iota(jnp.int32, (a.shape[0], b.shape[0]), 0)
        upto = lax.broadcasted_iota(jnp.int32, (a.shape[0], b.shape[0]), 1) <= at
        return jnp.where(upto, dot(a, b, ((1,), (1,))) * scale, 0.0).astype(BF16)

    for h in range(heads):
        cols = slice(h * HD, (h + 1) * HD)
        whole = slice((first + h) * HD, (first + h + 1) * HD)
        q, k, v, g = q_ref[:, whole], k_ref[:, whole], v_ref[:, whole], g_ref[:, whole]
        weights = causal(q[:cut], k[:cut], 0)
        scores = causal(g[:cut], v[:cut], 0)
        dq_ref[:cut, cols] = dot(scores, k[:cut], ((1,), (0,))).astype(BF16)
        dk = dot(scores, q[:cut], ((0,), (0,)))
        dv = dot(weights, g[:cut], ((0,), (0,)))
        if cut < rows:
            weights = causal(q[cut:], k, cut)
            scores = causal(g[cut:], v, cut)
            dq_ref[cut:, cols] = dot(scores, k, ((1,), (0,))).astype(BF16)
            low = dot(scores, q[cut:], ((0,), (0,)))
            dk, dk_ref[cut:, cols] = dk + low[:cut], low[cut:].astype(BF16)
            low = dot(weights, g[cut:], ((0,), (0,)))
            dv, dv_ref[cut:, cols] = dv + low[:cut], low[cut:].astype(BF16)
        dk_ref[:cut, cols] = dk.astype(BF16)
        dv_ref[:cut, cols] = dv.astype(BF16)


def within(arrays, first, heads, scale, after):
    rows = arrays[0].shape[0]
    return pl.pallas_call(
        functools.partial(within_kernel, first, heads, scale),
        out_shape=[jax.ShapeDtypeStruct((rows, heads * HD), BF16)] * 3,
        in_specs=[VMEM] * 4 + [ANY] * len(after),
        out_specs=[VMEM] * 3,
        compiler_params=pltpu.CompilerParams(vmem_limit_bytes=VMEM_LIMIT),
        cost_estimate=cost(heads * rows * HD, heads * rows * HD),
    )(*arrays, *after)


def diagonal(blocks):
    count = len(blocks)
    rows = [jnp.concatenate([b if j == i else jnp.zeros_like(b) for j in range(count)], axis=1) for i, b in enumerate(blocks)]
    return jnp.concatenate(rows, axis=0)


def final_kernel(first, half, scale, *refs):
    k_ref, v_ref, g_ref, other_ref, kept_ref, swapped_ref, gkept_ref, gswapped_ref = refs[:8]
    parts = refs[8:]
    piece = min(PIECE, 2 * half)
    buffers, sem, outs = refs[-4:-1], refs[-1], refs[-7:-4]
    later, second = place()
    per = 2 if half % 2 == 0 else 1
    copies = []
    for n in range(2 * half // per):
        upper = n * per >= half
        own = second if upper else jnp.logical_not(second)
        kv, qg = [], []
        for h in range(per):
            at = n * per % half + h
            here = jnp.where(own, kept_ref[at] + other_ref[at], swapped_ref[at] + other_ref[half + at])
            given = jnp.where(own, gswapped_ref[at], gkept_ref[at])
            kv.append(jnp.where(later, here, given).astype(BF16))
            qg.append(jnp.where(later, given, here).astype(BF16))
        kv, qg = diagonal(kv), diagonal(qg)
        cols = slice(n * per * HD, (n + 1) * per * HD)
        whole = slice((first + n * per) * HD, (first + (n + 1) * per) * HD)
        terms = (
            dot(g_ref[:, whole], kv, ((1,), (1,))),
            dot(v_ref[:, whole], qg, ((1,), (1,))),
            dot(k_ref[:, whole], qg, ((1,), (0,))),
        )
        held = slice(n * per % piece * HD, (n * per % piece + per) * HD)
        for j, term in enumerate(terms):
            part = parts[n * per // piece * 3 + j][:, held]
            buffers[j][:, cols] = (part.astype(F32) + scale * term).astype(BF16)
            copies.append(pltpu.make_async_copy(buffers[j].at[:, cols], outs[j].at[:, whole], sem.at[n, j]))
            copies[-1].start()
    for copy in copies:
        copy.wait()


def final(k, v, g, partials, other, states, first, size, scale, held):
    rows, width = k.shape
    return pl.pallas_call(
        functools.partial(final_kernel, first, size // 2, scale),
        out_shape=[jax.ShapeDtypeStruct((rows, width), BF16)] * 3,
        in_specs=[VMEM] * (8 + len(partials)) + [ANY] * len(held),
        out_specs=[ANY] * 3,
        scratch_shapes=[pltpu.VMEM((rows, size * HD), BF16)] * 3 + [pltpu.SemaphoreType.DMA((size, 3))],
        input_output_aliases={8 + len(partials) + j: j for j in range(len(held))},
        compiler_params=pltpu.CompilerParams(vmem_limit_bytes=VMEM_LIMIT),
        cost_estimate=cost(6 * size * rows * HD * HD, 18 * size * rows * HD),
    )(k, v, g, other, *states, *partials, *held)


def local(seq, queries, keys, values, out_grad):
    rows = queries.shape[0]
    heads = queries.shape[1] // HD
    scale = float(1.0 / (HD * rows * seq) ** 0.5)
    planes = seq // 4
    core_pairs = [(i, i ^ 1) for i in range(seq)]
    chip_pairs = [(i, i ^ 2) for i in range(seq)]

    def moved(value, plan):
        pairs = {}
        for to, source in plan.items():
            for chip in range(2):
                pairs[4 * source + 2 * chip + 1] = 4 * to + 2 * chip + 1
                pairs[4 * (planes - 1 - source) + 2 * chip] = 4 * (planes - 1 - to) + 2 * chip
        free = set(range(seq)) - set(pairs.values())
        for i in range(seq):
            if i not in pairs and i ^ 1 in free:
                pairs[i] = i ^ 1
                free.discard(i ^ 1)
        for chip in range(2):
            senders = [i for i in range(seq) if i not in pairs and i // 2 % 2 == chip]
            targets = [i for i in sorted(free) if i // 2 % 2 == chip]
            pairs.update(zip(senders, targets))
        return lax.ppermute(value, "seq", sorted(pairs.items()))

    def masked(total, values, plans):
        later, _ = place()
        plane = lax.axis_index("seq") // 4
        plane = jnp.where(later, plane, planes - 1 - plane)
        for value, plan in zip(values, plans):
            wanted = functools.reduce(jnp.logical_or, [plane == to for to in plan])
            total = total + jnp.where(wanted, value, 0.0)
        return total

    if planes == 4 and TREE:
        levels = [[{1: 0, 3: 2}], [{2: 1}, {3: 1}]]
    else:
        levels, by = [], 1
        while by < planes:
            levels.append([{to: to - j * by for to in range(j * by, planes)} for j in range(1, RADIX) if j * by < planes])
            by *= RADIX

    sizes = [heads * part // sum(CHUNKS) for part in CHUNKS]
    firsts = [sum(sizes[:i]) for i in range(len(sizes))]
    first_other, *arrays = first_state((queries, keys, values, out_grad), sizes[0])
    _, keys, values, out_grad = arrays
    chunks = range(len(sizes))
    made = {}
    pieces = [[] for _ in sizes]

    def wait_for(name, chunk):
        found = []
        for (c, p), after, before in PLACES:
            if before == (name, chunk):
                part = within(arrays, firsts[c] + p * PIECE, min(PIECE, sizes[c]), scale, [made[after]])
                pieces[c] = [*pieces[c], *part]
                found.append(part[0])
        return found

    for c in chunks:
        other = other_state(arrays, firsts[c], sizes[c]) if c else first_other
        made["other", c] = lax.ppermute(other, "seq", core_pairs)
    for c in chunks:
        made["kept", c], sent = chip_state(arrays, made["other", c], firsts[c], sizes[c])
        made["partner", c] = lax.ppermute(sent, "seq", chip_pairs)
    def stage(name, c, before):
        return wait_for(name, c) + ([made[before, c + 1]] if c + 1 < len(sizes) else [])

    for c in chunks:
        terms = [made["kept", c], made["partner", c]]
        (made["plane", c],) = sums(lambda a, b: (a + b,), 1, terms, stage("plane", c, "kept"))
        made["before", c] = None
    last = "plane"
    for number, plans in enumerate(levels[:-1]):
        name = f"window{number}"
        for c in chunks:

            def more(window, *arrived):
                add = masked(jnp.zeros_like(window), arrived[: len(plans)], plans)
                return window + add, sum(arrived[len(plans) :], add)

            window = made[last, c]
            arrived = [moved(window, plan) for plan in plans]
            held = [] if made["before", c] is None else [made["before", c]]
            made[name, c], made["before", c] = sums(more, 2, [window, *arrived, *held], stage(name, c, last))
        last = name

    done = []
    for c in chunks:
        plans = levels[-1]

        def ready(kept, partner, *arrived):
            _, second = place()
            total = masked(jnp.zeros_like(kept), arrived[: len(plans)], plans)
            total = sum(arrived[len(plans) :], total)
            return total + jnp.where(second, 0.0, kept), total + jnp.where(second, partner, 0.0)

        arrived = [moved(made[last, c], plan) for plan in plans]
        held = [] if made["before", c] is None else [made["before", c]]
        terms = [made["kept", c], made["partner", c], *arrived, *held]
        made["back", c], kept_upto = sums(ready, 2, terms, stage("scan", c, last))
        swapped = lax.ppermute(made["back", c], "seq", chip_pairs)
        done.append((made["other", c], kept_upto, swapped, lax.ppermute(kept_upto, "seq", core_pairs)))

    out, others = (), []
    for chunk, (first, size) in enumerate(zip(firsts, sizes)):
        other, kept_upto, swapped, given_kept = done[chunk]
        if chunk == len(sizes) - 1:
            swapped, given = lax.optimization_barrier((swapped, [d[3] for d in done] + others))
            done = [(*d[:3], g) for d, g in zip(done, given)]
            given_kept = done[chunk][3]
        given_swapped = lax.ppermute(swapped, "seq", core_pairs)
        others.append(given_swapped)
        ahead = [done[chunk + 1][2]] if chunk + 1 < len(sizes) else []
        given_swapped, ahead = lax.optimization_barrier((given_swapped, ahead))
        states = (kept_upto, swapped, given_kept, given_swapped)
        out = final(keys, values, out_grad, pieces[chunk], other, states, first, size, scale, out)
    return tuple(out)


def solution(mesh):
    spec = P(("groups", "seq"), None)
    return jax.shard_map(
        functools.partial(local, mesh.shape["seq"]),
        mesh=mesh,
        in_specs=(spec,) * 4,
        out_specs=(spec,) * 3,
        check_vma=False,
    )
```

```python
import functools

import jax
import jax.numpy as jnp
from jax import lax
from jax.experimental import pallas as pl
from jax.experimental.pallas import tpu as pltpu
from jax.sharding import PartitionSpec as P

HD = 128
CHUNKS = (8, 8)
RADIX = 2
TREE = True
PIECE = 4
PLACES = (
    ((0, 0), ("kept", 1), ("plane", 0)),
    ((0, 1), ("kept", 1), ("plane", 0)),
    ((1, 0), ("window0", 0), ("window0", 1)),
    ((1, 1), ("window0", 1), ("scan", 0)),
)
F32 = jnp.float32
BF16 = jnp.bfloat16
VMEM_LIMIT = 24 * 1024 * 1024
VMEM_FIRST = int(49.4 * 1024 * 1024)
VMEM_NEXT = int(47.4 * 1024 * 1024)
ANY = pl.BlockSpec(memory_space=pl.ANY)
HBM = pl.BlockSpec(memory_space=pltpu.HBM)
VMEM = pl.BlockSpec(memory_space=pltpu.VMEM)


def dot(a, b, dims):
    return lax.dot_general(a, b, (dims, ((), ())), preferred_element_type=F32)


def cost(flops, size):
    return pl.CostEstimate(flops=0, bytes_accessed=0, transcendentals=0)


def place():
    at = lax.axis_index("seq")
    core, chip = lax.rem(at, 2), lax.rem(at // 2, 2)
    return core == 1, core == chip


def load_kernel(first, size, count, q_ref, k_ref, v_ref, g_ref, *refs):
    other_ref, *targets, sem = refs[count:]
    later, second = place()
    half = size // 2

    def copies(j, source):
        made = []
        for n in range(2):
            cols = pl.ds((first + n * half) * HD, half * HD)
            target = targets[j].at[:, pl.ds(n * half * HD, half * HD)]
            made.append(pltpu.make_async_copy(source.at[:, cols], target, sem.at[j, n]))
        return made

    q, k, v, g = (copies(j, source) for j, source in enumerate((q_ref, k_ref, v_ref, g_ref)))

    def run(pair, refs, rest):
        for n in range(2):
            for copy in pair:
                copy[n].start()
        for n in range(2):
            for copy in rest:
                copy[n].start()
        turn = jnp.where(second, 0, half)
        for n in range(2):
            for copy in pair:
                copy[n].wait()
            for h in range(half):
                cols = slice((n * half + h) * HD, (n * half + h + 1) * HD)
                other_ref[lax.rem(n * half + turn, size) + h] = dot(refs[0][:, cols], refs[1][:, cols], ((0,), (0,)))
        for n in range(2):
            for copy in rest:
                copy[n].wait()

    qc_ref, kc_ref, vc_ref, gc_ref = targets

    @pl.when(later)
    def _():
        run((q, g), (qc_ref, gc_ref), (k, v))

    @pl.when(jnp.logical_not(later))
    def _():
        run((k, v), (kc_ref, vc_ref), (q, g))


def load(arrays, first, size, limit, after):
    rows = arrays[0].shape[0]
    return pl.pallas_call(
        functools.partial(load_kernel, first, size, len(after)),
        out_shape=[jax.ShapeDtypeStruct((size, HD, HD), F32)] + [jax.ShapeDtypeStruct((rows, size * HD), BF16)] * 4,
        in_specs=[ANY] * (4 + len(after)),
        out_specs=[VMEM] * 5,
        scratch_shapes=[pltpu.SemaphoreType.DMA((4, 2))],
        compiler_params=pltpu.CompilerParams(vmem_limit_bytes=limit),
        cost_estimate=cost(2 * size * rows * HD * HD, 16 * rows * size * HD),
    )(*arrays, *after)


def mine_kernel(size, q_ref, k_ref, v_ref, g_ref, other_ref, kept_ref, sent_ref):
    later, second = place()
    half = size // 2

    def run(pair, swap):
        refs = (sent_ref, kept_ref) if swap else (kept_ref, sent_ref)
        for h in range(size):
            cols = slice(h * HD, (h + 1) * HD)
            at = (h + (half if swap else 0)) % size
            value = dot(pair[0][:, cols], pair[1][:, cols], ((0,), (0,)))
            refs[h // half][h % half] = value + other_ref[at]

    for is_later, pair in ((True, (k_ref, v_ref)), (False, (q_ref, g_ref))):
        for swap in (True, False):
            pl.when(jnp.logical_and(later == is_later, second == swap))(functools.partial(run, pair, swap))


def chip_state(arrays, other, size):
    rows = arrays[0].shape[0]
    half = jax.ShapeDtypeStruct((size // 2, HD, HD), F32)
    return pl.pallas_call(
        functools.partial(mine_kernel, size),
        out_shape=[half, half],
        in_specs=[VMEM] * 5,
        out_specs=[VMEM, VMEM],
        compiler_params=pltpu.CompilerParams(vmem_limit_bytes=VMEM_LIMIT),
        cost_estimate=cost(2 * size * rows * HD * HD, 4 * size * rows * HD),
    )(*arrays, other)


def sums_kernel(count, outs, work, *refs):
    values = work(*[ref[...] for ref in refs[:count]])
    for ref, value in zip(refs[-outs:], values):
        ref[...] = value


def sums(work, outs, values, after=()):
    return pl.pallas_call(
        functools.partial(sums_kernel, len(values), outs, work),
        out_shape=[jax.ShapeDtypeStruct(values[0].shape, F32)] * outs,
        in_specs=[VMEM] * len(values) + [ANY] * len(after),
        out_specs=[VMEM] * outs,
        compiler_params=pltpu.CompilerParams(vmem_limit_bytes=VMEM_LIMIT),
        cost_estimate=cost(values[0].size, 8 * values[0].size),
    )(*values, *after)


def within_kernel(first, heads, scale, q_ref, k_ref, v_ref, g_ref, *refs):
    dq_ref, dk_ref, dv_ref = refs[-3:]
    rows = q_ref.shape[0]
    cut = 256 if rows > 256 else rows

    def causal(a, b, low):
        at = low + lax.broadcasted_iota(jnp.int32, (a.shape[0], b.shape[0]), 0)
        upto = lax.broadcasted_iota(jnp.int32, (a.shape[0], b.shape[0]), 1) <= at
        return jnp.where(upto, dot(a, b, ((1,), (1,))) * scale, 0.0).astype(BF16)

    for h in range(heads):
        cols = slice(h * HD, (h + 1) * HD)
        whole = slice((first + h) * HD, (first + h + 1) * HD)
        q, k, v, g = q_ref[:, whole], k_ref[:, whole], v_ref[:, whole], g_ref[:, whole]
        weights = causal(q[:cut], k[:cut], 0)
        scores = causal(g[:cut], v[:cut], 0)
        dq_ref[:cut, cols] = dot(scores, k[:cut], ((1,), (0,))).astype(BF16)
        dk = dot(scores, q[:cut], ((0,), (0,)))
        dv = dot(weights, g[:cut], ((0,), (0,)))
        if cut < rows:
            weights = causal(q[cut:], k, cut)
            scores = causal(g[cut:], v, cut)
            dq_ref[cut:, cols] = dot(scores, k, ((1,), (0,))).astype(BF16)
            low = dot(scores, q[cut:], ((0,), (0,)))
            dk, dk_ref[cut:, cols] = dk + low[:cut], low[cut:].astype(BF16)
            low = dot(weights, g[cut:], ((0,), (0,)))
            dv, dv_ref[cut:, cols] = dv + low[:cut], low[cut:].astype(BF16)
        dk_ref[:cut, cols] = dk.astype(BF16)
        dv_ref[:cut, cols] = dv.astype(BF16)


def within(arrays, first, heads, scale, after):
    rows = arrays[0].shape[0]
    return pl.pallas_call(
        functools.partial(within_kernel, first, heads, scale),
        out_shape=[jax.ShapeDtypeStruct((rows, heads * HD), BF16)] * 3,
        in_specs=[VMEM] * 4 + [ANY] * len(after),
        out_specs=[VMEM] * 3,
        compiler_params=pltpu.CompilerParams(vmem_limit_bytes=VMEM_LIMIT),
        cost_estimate=cost(heads * rows * HD, heads * rows * HD),
    )(*arrays, *after)


def diagonal(blocks):
    count = len(blocks)
    rows = [jnp.concatenate([b if j == i else jnp.zeros_like(b) for j in range(count)], axis=1) for i, b in enumerate(blocks)]
    return jnp.concatenate(rows, axis=0)


def final_kernel(first, half, scale, *refs):
    k_ref, v_ref, g_ref, other_ref, kept_ref, swapped_ref, gkept_ref, gswapped_ref = refs[:8]
    parts = refs[8:]
    piece = min(PIECE, 2 * half)
    buffers, sem, outs = refs[-4:-1], refs[-1], refs[-7:-4]
    later, second = place()
    per = 2 if half % 2 == 0 else 1
    copies = []
    for n in range(2 * half // per):
        upper = n * per >= half
        own = second if upper else jnp.logical_not(second)
        kv, qg = [], []
        for h in range(per):
            at = n * per % half + h
            here = jnp.where(own, kept_ref[at] + other_ref[at], swapped_ref[at] + other_ref[half + at])
            given = jnp.where(own, gswapped_ref[at], gkept_ref[at])
            kv.append(jnp.where(later, here, given).astype(BF16))
            qg.append(jnp.where(later, given, here).astype(BF16))
        kv, qg = diagonal(kv), diagonal(qg)
        cols = slice(n * per * HD, (n + 1) * per * HD)
        whole = slice((first + n * per) * HD, (first + (n + 1) * per) * HD)
        terms = (
            dot(g_ref[:, cols], kv, ((1,), (1,))),
            dot(v_ref[:, cols], qg, ((1,), (1,))),
            dot(k_ref[:, cols], qg, ((1,), (0,))),
        )
        held = slice(n * per % piece * HD, (n * per % piece + per) * HD)
        for j, term in enumerate(terms):
            part = parts[n * per // piece * 3 + j][:, held]
            buffers[j][:, cols] = (part.astype(F32) + scale * term).astype(BF16)
            copies.append(pltpu.make_async_copy(buffers[j].at[:, cols], outs[j].at[:, whole], sem.at[n, j]))
            copies[-1].start()
    for copy in copies:
        copy.wait()


def final(k, v, g, partials, other, states, first, size, width, scale, held):
    rows = k.shape[0]
    return pl.pallas_call(
        functools.partial(final_kernel, first, size // 2, scale),
        out_shape=[jax.ShapeDtypeStruct((rows, width), BF16)] * 3,
        in_specs=[VMEM] * (8 + len(partials)) + [ANY] * len(held),
        out_specs=[ANY] * 3,
        scratch_shapes=[pltpu.VMEM((rows, size * HD), BF16)] * 3 + [pltpu.SemaphoreType.DMA((size, 3))],
        input_output_aliases={8 + len(partials) + j: j for j in range(len(held))},
        compiler_params=pltpu.CompilerParams(vmem_limit_bytes=VMEM_LIMIT),
        cost_estimate=cost(6 * size * rows * HD * HD, 18 * size * rows * HD),
    )(k, v, g, other, *states, *partials, *held)


def local(seq, queries, keys, values, out_grad):
    rows = queries.shape[0]
    heads = queries.shape[1] // HD
    scale = float(1.0 / (HD * rows * seq) ** 0.5)
    planes = seq // 4
    core_pairs = [(i, i ^ 1) for i in range(seq)]
    chip_pairs = [(i, i ^ 2) for i in range(seq)]

    def moved(value, plan):
        pairs = {}
        for to, source in plan.items():
            for chip in range(2):
                pairs[4 * source + 2 * chip + 1] = 4 * to + 2 * chip + 1
                pairs[4 * (planes - 1 - source) + 2 * chip] = 4 * (planes - 1 - to) + 2 * chip
        free = set(range(seq)) - set(pairs.values())
        for i in range(seq):
            if i not in pairs and i ^ 1 in free:
                pairs[i] = i ^ 1
                free.discard(i ^ 1)
        for chip in range(2):
            senders = [i for i in range(seq) if i not in pairs and i // 2 % 2 == chip]
            targets = [i for i in sorted(free) if i // 2 % 2 == chip]
            pairs.update(zip(senders, targets))
        return lax.ppermute(value, "seq", sorted(pairs.items()))

    def masked(total, values, plans):
        later, _ = place()
        plane = lax.axis_index("seq") // 4
        plane = jnp.where(later, plane, planes - 1 - plane)
        for value, plan in zip(values, plans):
            wanted = functools.reduce(jnp.logical_or, [plane == to for to in plan])
            total = total + jnp.where(wanted, value, 0.0)
        return total

    if planes == 4 and TREE:
        levels = [[{1: 0, 3: 2}], [{3: 1}, {2: 1}]]
    else:
        levels, by = [], 1
        while by < planes:
            levels.append([{to: to - j * by for to in range(j * by, planes)} for j in range(1, RADIX) if j * by < planes])
            by *= RADIX

    sizes = [heads * part // sum(CHUNKS) for part in CHUNKS]
    firsts = [sum(sizes[:i]) for i in range(len(sizes))]
    chunks = range(len(sizes))
    made = {}
    pieces = [[] for _ in sizes]

    def wait_for(name, chunk):
        found = []
        for (c, p), after, before in PLACES:
            if before == (name, chunk):
                part = within(made["arrays", c], p * PIECE, min(PIECE, sizes[c]), scale, [made[after]])
                pieces[c] = [*pieces[c], *part]
                found.append(part[0])
        return found

    for c in chunks:
        after = [made["sum", c - 1]] if c else []
        limit = VMEM_FIRST if c == 0 else VMEM_NEXT
        other, *made["arrays", c] = load((queries, keys, values, out_grad), firsts[c], sizes[c], limit, after)
        made["sum", c] = other
        made["other", c] = lax.ppermute(other, "seq", core_pairs)
        made["kept", c], sent = chip_state(made["arrays", c], made["other", c], sizes[c])
        made["partner", c] = lax.ppermute(sent, "seq", chip_pairs)

    def stage(name, c, before):
        return wait_for(name, c) + ([made[before, c + 1]] if c + 1 < len(sizes) else [])

    for c in chunks:
        terms = [made["kept", c], made["partner", c]]
        (made["plane", c],) = sums(lambda a, b: (a + b,), 1, terms, stage("plane", c, "kept"))
        made["before", c] = None
    last = "plane"
    for number, plans in enumerate(levels[:-1]):
        name = f"window{number}"
        for c in chunks:

            def more(window, *arrived):
                add = masked(jnp.zeros_like(window), arrived[: len(plans)], plans)
                return window + add, sum(arrived[len(plans) :], add)

            window = made[last, c]
            arrived = [moved(window, plan) for plan in plans]
            held = [] if made["before", c] is None else [made["before", c]]
            made[name, c], made["before", c] = sums(more, 2, [window, *arrived, *held], stage(name, c, last))
        last = name

    done = []
    for c in chunks:
        plans = levels[-1]

        def ready(kept, partner, *arrived):
            _, second = place()
            total = masked(jnp.zeros_like(kept), arrived[: len(plans)], plans)
            total = sum(arrived[len(plans) :], total)
            return total + jnp.where(second, 0.0, kept), total + jnp.where(second, partner, 0.0)

        arrived = [moved(made[last, c], plan) for plan in plans]
        held = [] if made["before", c] is None else [made["before", c]]
        terms = [made["kept", c], made["partner", c], *arrived, *held]
        made["back", c], kept_upto = sums(ready, 2, terms, stage("scan", c, last))
        swapped = lax.ppermute(made["back", c], "seq", chip_pairs)
        done.append((made["other", c], kept_upto, swapped, lax.ppermute(kept_upto, "seq", core_pairs)))

    out, others = (), []
    for chunk, (first, size) in enumerate(zip(firsts, sizes)):
        other, kept_upto, swapped, given_kept = done[chunk]
        if chunk == len(sizes) - 1:
            swapped, given = lax.optimization_barrier((swapped, [d[3] for d in done] + others))
            done = [(*d[:3], g) for d, g in zip(done, given)]
            given_kept = done[chunk][3]
        given_swapped = lax.ppermute(swapped, "seq", core_pairs)
        others.append(given_swapped)
        ahead = [done[chunk + 1][2]] if chunk + 1 < len(sizes) else []
        given_swapped, ahead = lax.optimization_barrier((given_swapped, ahead))
        states = (kept_upto, swapped, given_kept, given_swapped)
        out = final(*made["arrays", chunk][1:], pieces[chunk], other, states, first, size, heads * HD, scale, out)
    return tuple(out)


def solution(mesh):
    spec = P(("groups", "seq"), None)
    return jax.shard_map(
        functools.partial(local, mesh.shape["seq"]),
        mesh=mesh,
        in_specs=(spec,) * 4,
        out_specs=(spec,) * 3,
        check_vma=False,
    )
```

```python
import functools

import jax
import jax.numpy as jnp
from jax import lax
from jax.experimental import pallas as pl
from jax.experimental.pallas import tpu as pltpu
from jax.sharding import PartitionSpec as P

HD = 128
CHUNKS = (8, 8)
RADIX = 2
TREE = True
PIECE = 4
PLACES = (
    ((0, 0), ("kept", 1), ("plane", 0)),
    ((0, 1), ("kept", 1), ("plane", 0)),
    ((1, 0), ("window0", 0), ("window0", 1)),
    ((1, 1), ("back", 0), ("scan", 1)),
)
F32 = jnp.float32
BF16 = jnp.bfloat16
VMEM_LIMIT = 24 * 1024 * 1024
VMEM_FIRST = int(49.4 * 1024 * 1024)
VMEM_NEXT = int(47.4 * 1024 * 1024)
ANY = pl.BlockSpec(memory_space=pl.ANY)
HBM = pl.BlockSpec(memory_space=pltpu.HBM)
VMEM = pl.BlockSpec(memory_space=pltpu.VMEM)


def dot(a, b, dims):
    return lax.dot_general(a, b, (dims, ((), ())), preferred_element_type=F32)


def cost(flops, size):
    return pl.CostEstimate(flops=0, bytes_accessed=0, transcendentals=0)


def place():
    at = lax.axis_index("seq")
    core, chip = lax.rem(at, 2), lax.rem(at // 2, 2)
    return core == 1, core == chip


def load_kernel(first, size, count, q_ref, k_ref, v_ref, g_ref, *refs):
    other_ref, *targets, sem = refs[count:]
    later, second = place()
    half = size // 2

    def copies(j, source):
        made = []
        for n in range(2):
            cols = pl.ds((first + n * half) * HD, half * HD)
            target = targets[j].at[:, pl.ds(n * half * HD, half * HD)]
            made.append(pltpu.make_async_copy(source.at[:, cols], target, sem.at[j, n]))
        return made

    q, k, v, g = (copies(j, source) for j, source in enumerate((q_ref, k_ref, v_ref, g_ref)))

    def run(pair, refs, rest):
        for n in range(2):
            for copy in pair:
                copy[n].start()
        for n in range(2):
            for copy in rest:
                copy[n].start()
        turn = jnp.where(second, 0, half)
        for n in range(2):
            for copy in pair:
                copy[n].wait()
            for h in range(half):
                cols = slice((n * half + h) * HD, (n * half + h + 1) * HD)
                other_ref[lax.rem(n * half + turn, size) + h] = dot(refs[0][:, cols], refs[1][:, cols], ((0,), (0,)))
        for n in range(2):
            for copy in rest:
                copy[n].wait()

    qc_ref, kc_ref, vc_ref, gc_ref = targets

    @pl.when(later)
    def _():
        run((q, g), (qc_ref, gc_ref), (k, v))

    @pl.when(jnp.logical_not(later))
    def _():
        run((k, v), (kc_ref, vc_ref), (q, g))


def load(arrays, first, size, limit, after):
    rows = arrays[0].shape[0]
    return pl.pallas_call(
        functools.partial(load_kernel, first, size, len(after)),
        out_shape=[jax.ShapeDtypeStruct((size, HD, HD), F32)] + [jax.ShapeDtypeStruct((rows, size * HD), BF16)] * 4,
        in_specs=[ANY] * (4 + len(after)),
        out_specs=[VMEM] * 5,
        scratch_shapes=[pltpu.SemaphoreType.DMA((4, 2))],
        compiler_params=pltpu.CompilerParams(vmem_limit_bytes=limit),
        cost_estimate=cost(2 * size * rows * HD * HD, 16 * rows * size * HD),
    )(*arrays, *after)


def mine_kernel(size, q_ref, k_ref, v_ref, g_ref, other_ref, kept_ref, sent_ref):
    later, second = place()
    half = size // 2

    def run(pair, swap):
        refs = (sent_ref, kept_ref) if swap else (kept_ref, sent_ref)
        for h in range(size):
            cols = slice(h * HD, (h + 1) * HD)
            at = (h + (half if swap else 0)) % size
            value = dot(pair[0][:, cols], pair[1][:, cols], ((0,), (0,)))
            refs[h // half][h % half] = value + other_ref[at]

    for is_later, pair in ((True, (k_ref, v_ref)), (False, (q_ref, g_ref))):
        for swap in (True, False):
            pl.when(jnp.logical_and(later == is_later, second == swap))(functools.partial(run, pair, swap))


def chip_state(arrays, other, size):
    rows = arrays[0].shape[0]
    half = jax.ShapeDtypeStruct((size // 2, HD, HD), F32)
    return pl.pallas_call(
        functools.partial(mine_kernel, size),
        out_shape=[half, half],
        in_specs=[VMEM] * 5,
        out_specs=[VMEM, VMEM],
        compiler_params=pltpu.CompilerParams(vmem_limit_bytes=VMEM_LIMIT),
        cost_estimate=cost(2 * size * rows * HD * HD, 4 * size * rows * HD),
    )(*arrays, other)


def sums_kernel(count, outs, work, *refs):
    values = work(*[ref[...] for ref in refs[:count]])
    for ref, value in zip(refs[-outs:], values):
        ref[...] = value


def sums(work, outs, values, after=()):
    return pl.pallas_call(
        functools.partial(sums_kernel, len(values), outs, work),
        out_shape=[jax.ShapeDtypeStruct(values[0].shape, F32)] * outs,
        in_specs=[VMEM] * len(values) + [ANY] * len(after),
        out_specs=[VMEM] * outs,
        compiler_params=pltpu.CompilerParams(vmem_limit_bytes=VMEM_LIMIT),
        cost_estimate=cost(values[0].size, 8 * values[0].size),
    )(*values, *after)


def within_kernel(first, heads, scale, q_ref, k_ref, v_ref, g_ref, *refs):
    dq_ref, dk_ref, dv_ref = refs[-3:]
    rows = q_ref.shape[0]
    cut = 256 if rows > 256 else rows

    def causal(a, b, low):
        at = low + lax.broadcasted_iota(jnp.int32, (a.shape[0], b.shape[0]), 0)
        upto = lax.broadcasted_iota(jnp.int32, (a.shape[0], b.shape[0]), 1) <= at
        return jnp.where(upto, dot(a, b, ((1,), (1,))) * scale, 0.0).astype(BF16)

    for h in range(heads):
        cols = slice(h * HD, (h + 1) * HD)
        whole = slice((first + h) * HD, (first + h + 1) * HD)
        q, k, v, g = q_ref[:, whole], k_ref[:, whole], v_ref[:, whole], g_ref[:, whole]
        weights = causal(q[:cut], k[:cut], 0)
        scores = causal(g[:cut], v[:cut], 0)
        dq_ref[:cut, cols] = dot(scores, k[:cut], ((1,), (0,))).astype(BF16)
        dk = dot(scores, q[:cut], ((0,), (0,)))
        dv = dot(weights, g[:cut], ((0,), (0,)))
        if cut < rows:
            weights = causal(q[cut:], k, cut)
            scores = causal(g[cut:], v, cut)
            dq_ref[cut:, cols] = dot(scores, k, ((1,), (0,))).astype(BF16)
            low = dot(scores, q[cut:], ((0,), (0,)))
            dk, dk_ref[cut:, cols] = dk + low[:cut], low[cut:].astype(BF16)
            low = dot(weights, g[cut:], ((0,), (0,)))
            dv, dv_ref[cut:, cols] = dv + low[:cut], low[cut:].astype(BF16)
        dk_ref[:cut, cols] = dk.astype(BF16)
        dv_ref[:cut, cols] = dv.astype(BF16)


def within(arrays, first, heads, scale, after):
    rows = arrays[0].shape[0]
    return pl.pallas_call(
        functools.partial(within_kernel, first, heads, scale),
        out_shape=[jax.ShapeDtypeStruct((rows, heads * HD), BF16)] * 3,
        in_specs=[VMEM] * 4 + [ANY] * len(after),
        out_specs=[VMEM] * 3,
        compiler_params=pltpu.CompilerParams(vmem_limit_bytes=VMEM_LIMIT),
        cost_estimate=cost(heads * rows * HD, heads * rows * HD),
    )(*arrays, *after)


def diagonal(blocks):
    count = len(blocks)
    rows = [jnp.concatenate([b if j == i else jnp.zeros_like(b) for j in range(count)], axis=1) for i, b in enumerate(blocks)]
    return jnp.concatenate(rows, axis=0)


def final_kernel(first, half, scale, *refs):
    k_ref, v_ref, g_ref, other_ref, kept_ref, swapped_ref, gkept_ref, gswapped_ref = refs[:8]
    parts = refs[8:]
    piece = min(PIECE, 2 * half)
    buffers, sem, outs = refs[-4:-1], refs[-1], refs[-7:-4]
    later, second = place()
    per = 2 if half % 2 == 0 else 1
    copies = []
    for n in range(2 * half // per):
        upper = n * per >= half
        own = second if upper else jnp.logical_not(second)
        kv, qg = [], []
        for h in range(per):
            at = n * per % half + h
            here = jnp.where(own, kept_ref[at] + other_ref[at], swapped_ref[at] + other_ref[half + at])
            given = jnp.where(own, gswapped_ref[at], gkept_ref[at])
            kv.append(jnp.where(later, here, given).astype(BF16))
            qg.append(jnp.where(later, given, here).astype(BF16))
        kv, qg = diagonal(kv), diagonal(qg)
        cols = slice(n * per * HD, (n + 1) * per * HD)
        whole = slice((first + n * per) * HD, (first + (n + 1) * per) * HD)
        terms = (
            dot(g_ref[:, cols], kv, ((1,), (1,))),
            dot(v_ref[:, cols], qg, ((1,), (1,))),
            dot(k_ref[:, cols], qg, ((1,), (0,))),
        )
        held = slice(n * per % piece * HD, (n * per % piece + per) * HD)
        for j, term in enumerate(terms):
            part = parts[n * per // piece * 3 + j][:, held]
            buffers[j][:, cols] = (part.astype(F32) + scale * term).astype(BF16)
            copies.append(pltpu.make_async_copy(buffers[j].at[:, cols], outs[j].at[:, whole], sem.at[n, j]))
            copies[-1].start()
    for copy in copies:
        copy.wait()


def final(k, v, g, partials, other, states, first, size, width, scale, held):
    rows = k.shape[0]
    return pl.pallas_call(
        functools.partial(final_kernel, first, size // 2, scale),
        out_shape=[jax.ShapeDtypeStruct((rows, width), BF16)] * 3,
        in_specs=[VMEM] * (8 + len(partials)) + [ANY] * len(held),
        out_specs=[ANY] * 3,
        scratch_shapes=[pltpu.VMEM((rows, size * HD), BF16)] * 3 + [pltpu.SemaphoreType.DMA((size, 3))],
        input_output_aliases={8 + len(partials) + j: j for j in range(len(held))},
        compiler_params=pltpu.CompilerParams(vmem_limit_bytes=VMEM_LIMIT),
        cost_estimate=cost(6 * size * rows * HD * HD, 18 * size * rows * HD),
    )(k, v, g, other, *states, *partials, *held)


def local(seq, queries, keys, values, out_grad):
    rows = queries.shape[0]
    heads = queries.shape[1] // HD
    scale = float(1.0 / (HD * rows * seq) ** 0.5)
    planes = seq // 4
    core_pairs = [(i, i ^ 1) for i in range(seq)]
    chip_pairs = [(i, i ^ 2) for i in range(seq)]

    def moved(value, plan):
        pairs = {}
        for to, source in plan.items():
            for chip in range(2):
                pairs[4 * source + 2 * chip + 1] = 4 * to + 2 * chip + 1
                pairs[4 * (planes - 1 - source) + 2 * chip] = 4 * (planes - 1 - to) + 2 * chip
        free = set(range(seq)) - set(pairs.values())
        for i in range(seq):
            if i not in pairs and i ^ 1 in free:
                pairs[i] = i ^ 1
                free.discard(i ^ 1)
        for chip in range(2):
            senders = [i for i in range(seq) if i not in pairs and i // 2 % 2 == chip]
            targets = [i for i in sorted(free) if i // 2 % 2 == chip]
            pairs.update(zip(senders, targets))
        return lax.ppermute(value, "seq", sorted(pairs.items()))

    def masked(total, values, plans):
        later, _ = place()
        plane = lax.axis_index("seq") // 4
        plane = jnp.where(later, plane, planes - 1 - plane)
        for value, plan in zip(values, plans):
            wanted = functools.reduce(jnp.logical_or, [plane == to for to in plan])
            total = total + jnp.where(wanted, value, 0.0)
        return total

    if planes == 4 and TREE:
        levels = [[{1: 0, 3: 2}], [{3: 1}, {2: 1}]]
    else:
        levels, by = [], 1
        while by < planes:
            levels.append([{to: to - j * by for to in range(j * by, planes)} for j in range(1, RADIX) if j * by < planes])
            by *= RADIX

    sizes = [heads * part // sum(CHUNKS) for part in CHUNKS]
    firsts = [sum(sizes[:i]) for i in range(len(sizes))]
    chunks = range(len(sizes))
    made = {}
    pieces = [[] for _ in sizes]

    def wait_for(name, chunk):
        found = []
        for (c, p), after, before in PLACES:
            if before == (name, chunk):
                part = within(made["arrays", c], p * PIECE, min(PIECE, sizes[c]), scale, [made[after]])
                pieces[c] = [*pieces[c], *part]
                found.append(part[0])
        return found

    for c in chunks:
        after = [made["sum", c - 1]] if c else []
        limit = VMEM_FIRST if c == 0 else VMEM_NEXT
        other, *made["arrays", c] = load((queries, keys, values, out_grad), firsts[c], sizes[c], limit, after)
        made["sum", c] = other
        made["other", c] = lax.ppermute(other, "seq", core_pairs)
        made["kept", c], sent = chip_state(made["arrays", c], made["other", c], sizes[c])
        made["partner", c] = lax.ppermute(sent, "seq", chip_pairs)

    def stage(name, c, before):
        return wait_for(name, c) + ([made[before, c + 1]] if c + 1 < len(sizes) else [])

    for c in chunks:
        terms = [made["kept", c], made["partner", c]]
        (made["plane", c],) = sums(lambda a, b: (a + b,), 1, terms, stage("plane", c, "kept"))
        made["before", c] = None
    last = "plane"
    for number, plans in enumerate(levels[:-1]):
        name = f"window{number}"
        for c in chunks:

            def more(window, kept, *arrived):
                _, second = place()
                add = masked(jnp.zeros_like(window), arrived[: len(plans)], plans)
                total = sum(arrived[len(plans) :], add)
                return window + add, total, total + jnp.where(second, 0.0, kept)

            window = made[last, c]
            arrived = [moved(window, plan) for plan in plans]
            held = [] if made["before", c] is None else [made["before", c]]
            terms = [window, made["kept", c], *arrived, *held]
            made[name, c], made["before", c], made["early", c] = sums(more, 3, terms, stage(name, c, last))
        last = name

    needing = set().union(*levels[-1])
    late_pairs = []
    for i in range(seq):
        plane = i // 4 if i % 2 else planes - 1 - i // 4
        beside = i // 4 + (1 if (plane % 2 == 0) == (i % 2 == 1) else -1)
        late_pairs.append((i, i ^ 2 if plane in needing else 4 * beside + i % 4))

    def is_late():
        later, _ = place()
        plane = lax.axis_index("seq") // 4
        plane = jnp.where(later, plane, planes - 1 - plane)
        return functools.reduce(jnp.logical_or, [plane == to for to in needing])

    early = [lax.ppermute(made["early", c], "seq", chip_pairs) for c in chunks]
    done = []
    for c in chunks:
        plans = levels[-1][:: -1 if c else 1]

        def ready(kept, partner, *arrived):
            _, second = place()
            total = masked(jnp.zeros_like(kept), arrived[: len(plans)], plans)
            total = sum(arrived[len(plans) :], total)
            return total + jnp.where(second, 0.0, kept), total + jnp.where(second, partner, 0.0)

        arrived = [moved(made[last, c], plan) for plan in plans]
        held = [] if made["before", c] is None else [made["before", c]]
        terms = [made["kept", c], made["partner", c], *arrived, *held]
        made["back", c], kept_upto = sums(ready, 2, terms, stage("scan", c, last) + [early[c]])
        late = lax.ppermute(made["back", c], "seq", late_pairs)
        (swapped,) = sums(lambda late, early: (jnp.where(is_late(), late, early),), 1, [late, early[c]])
        done.append((made["other", c], kept_upto, swapped, lax.ppermute(kept_upto, "seq", core_pairs)))

    out, others = (), []
    for chunk, (first, size) in enumerate(zip(firsts, sizes)):
        other, kept_upto, swapped, given_kept = done[chunk]
        if chunk == len(sizes) - 1:
            swapped, given = lax.optimization_barrier((swapped, [d[3] for d in done] + others))
            done = [(*d[:3], g) for d, g in zip(done, given)]
            given_kept = done[chunk][3]
        given_swapped = lax.ppermute(swapped, "seq", core_pairs)
        others.append(given_swapped)
        ahead = [done[chunk + 1][2]] if chunk + 1 < len(sizes) else []
        given_swapped, ahead = lax.optimization_barrier((given_swapped, ahead))
        states = (kept_upto, swapped, given_kept, given_swapped)
        out = final(*made["arrays", chunk][1:], pieces[chunk], other, states, first, size, heads * HD, scale, out)
    return tuple(out)


def solution(mesh):
    spec = P(("groups", "seq"), None)
    return jax.shard_map(
        functools.partial(local, mesh.shape["seq"]),
        mesh=mesh,
        in_specs=(spec,) * 4,
        out_specs=(spec,) * 3,
        check_vma=False,
    )
```
